32 devices in a mesh: head: 8 (over z, y), seq: 4 (over x, core).
Axes of the slice: x: 2, y: 2, z: 4, core: 2. Of those that a mesh axis runs over, the one named last changes fastest.
Arguments:
- query_rows: bfloat16 [2, 2048, 4096], P(None, ('seq', 'head')), may hold values from -6 to 6
- key_rows: bfloat16 [2, 2048, 4096], P(None, ('seq', 'head')), may hold values from -6 to 6
- value_rows: bfloat16 [2, 2048, 4096], P(None, ('seq', 'head')), may hold values from -6 to 6
- beta_raw: bfloat16 [2, 2048, 32], P(None, ('seq', 'head')), may hold values from -5 to 5
- gate_latent: bfloat16 [2, 2048, 128], P(None, ('seq', 'head')), may hold values from -3 to 3
- gate_up: bfloat16 [128, 4096], replicated, may hold values from -1 to 1
- dt_bias: float32 [2, 4096], replicated, may hold values from -13 to -1
- decay_log: float32 [32], replicated, may hold values from -0.5 to 0.5
- boundary: int32 [2, 2048], P(None, ('seq', 'head')), may hold values 0 or 1
- modality: int32 [2, 2048], P(None, ('seq', 'head')), may hold values from 0 to 1, as said below
- out_gate: bfloat16 [2, 2048, 4096], P(None, ('seq', 'head')), may hold values from -6 to 6
- norm_gain: float32 [4096], replicated, may hold values from 0.1 to 1.9
Outputs:
- mixed_out: bfloat16 [2, 2048, 4096], P(None, ('seq', 'head'))
The draws below stay inside these ranges and needn't reach their ends.
Inputs may be any that keep to these rules, and one draw needn't show every extreme that they name: `modality`: each sequence has runs of audio and runs of text; the value changes at a few positions.
All inputs are finite; a program needn't handle non-finite values. No bound on the sum of `boundary` on one device may be relied on, other than what follows from the above.
Results may differ from the reference program's by a relative error of at most 0.0049.
Values may be sent and summed in bfloat16 or wider, within the bound.
No kernel may reach another device: no remote copies, remote signals or barrier semaphores. Data moves between devices by JAX's collectives and lax.ppermute only.
A program may use at most 128 MiB of HBM per device.

```python
import math
import jax
import jax.numpy as jnp
from jax import lax

H = 32
DK = 128
RANK = 128
BATCH = 2
BLOCK = 128
LENGTH = 2048
HD = 4096


def draw_gate_up(key, part):
    normal_raw = jax.random.normal(key, (RANK, H * DK), jnp.float32)
    return (jnp.clip(normal_raw, -3.0, 3.0) * (0.5 / math.sqrt(RANK))).astype(jnp.bfloat16)


def draw_dt_bias(key, part):
    key_pick, key_fast, key_slow, key_text = jax.random.split(jax.random.fold_in(key, 11), 4)
    columns = H * DK
    slow_share = 0.5
    selector = jax.random.uniform(key_pick, (columns,))
    fast_rate = jnp.exp(jax.random.uniform(key_fast, (columns,), minval=math.log(1.0 / 64.0), maxval=math.log(1.0 / 16.0)))
    slow_rate = jnp.exp(jax.random.uniform(key_slow, (columns,), minval=math.log(0.1), maxval=math.log(0.5))) / LENGTH
    rates = jnp.where(selector < slow_share, slow_rate, fast_rate)
    audio_row = jnp.log(jnp.expm1(rates))
    text_row = audio_row + jnp.log(jax.random.uniform(key_text, (columns,), minval=1.5, maxval=3.0))
    return jnp.stack([audio_row, text_row]).astype(jnp.float32)


def draw_modality(key, part):
    key_ticks, key_start = jax.random.split(jax.random.fold_in(key, 23))
    random_ticks = jax.random.randint(key_ticks, (BATCH, LENGTH), 0, LENGTH)
    switch_mask = (random_ticks < 16).astype(jnp.int32)
    midpoint = (lax.broadcasted_iota(jnp.int32, (BATCH, LENGTH), 1) == LENGTH // 2).astype(jnp.int32)
    opening = jax.random.randint(key_start, (BATCH, 1), 0, 2)
    return (jnp.cumsum(jnp.maximum(switch_mask, midpoint), axis=1) + opening) % 2


def place_ends(entries, rng, low, largest):
    longest = entries.shape.index(max(entries.shape))
    spots = []
    for shift in (0, 1):
        where = [jax.random.randint(jax.random.fold_in(rng, axis), (), 0, length) for axis, length in enumerate(entries.shape)]
        where[longest] = (where[longest] + shift) % entries.shape[longest]
        spots.append(tuple(where))
    return entries.at[spots[0]].set(low).at[spots[1]].set(largest)


def shard_levels(rng, dims, cuts, low, largest):
    loudness, own = 1.0, jax.random.fold_in(rng, 6)
    for position, parts in cuts:
        heights = jnp.exp(jax.random.uniform(jax.random.fold_in(own, position), (parts,), jnp.float32, low / len(cuts), largest / len(cuts)))
        loudness = loudness * jnp.repeat(heights, dims[position] // parts).reshape([-1 if axis == position else 1 for axis in range(len(dims))])
    return loudness


def gaussian(own_key, dims, spread, bound, cuts=(), kind=jnp.bfloat16):
    values = jax.random.normal(own_key, dims, jnp.float32) * spread
    if len(cuts) > 0:
        values = shard_levels(own_key, dims, cuts, -0.22, 0.18) * values
    return jnp.clip(values, min=-bound, max=bound).astype(kind)


def setup_inputs(seed: int = 0) -> dict:
    key_list = jax.random.split(jax.random.key(seed), 13)
    query_rows = gaussian(key_list[0], (BATCH, LENGTH, HD), 1.0, 6.0, ((1, 32),))
    key_rows = gaussian(key_list[1], (BATCH, LENGTH, HD), 1.0, 6.0, ((1, 32),))
    value_rows = gaussian(key_list[2], (BATCH, LENGTH, HD), 1.0, 6.0, ((1, 32),))
    beta_raw = gaussian(key_list[3], (BATCH, LENGTH, H), 1.0, 5.0, ((1, 32),))
    gate_latent = gaussian(key_list[4], (BATCH, LENGTH, RANK), 1.0, 3.0, ((1, 32),))
    gate_up = draw_gate_up(jax.random.fold_in(key_list[12], 71), 0)
    dt_bias = draw_dt_bias(jax.random.fold_in(key_list[12], 71), 0)
    decay_log = jnp.clip(jax.random.uniform(key_list[7], (H,), jnp.float32, -0.5, 0.5), -0.5, 0.5)
    boundary = place_ends((jax.random.randint(key_list[8], (BATCH, LENGTH), 0, LENGTH) < 2).astype(jnp.int32), jax.random.fold_in(key_list[8], 1), 0, 1)
    modality = draw_modality(jax.random.fold_in(key_list[12], 71), 0)
    out_gate = gaussian(key_list[10], (BATCH, LENGTH, HD), 1.0, 6.0, ((1, 32),))
    norm_gain = jnp.clip(1.0 + 0.18 * jax.random.normal(key_list[11], (HD,), jnp.float32), 0.1, 1.9)
    return dict(query_rows=query_rows, key_rows=key_rows, value_rows=value_rows, beta_raw=beta_raw, gate_latent=gate_latent, gate_up=gate_up, dt_bias=dt_bias, decay_log=decay_log, boundary=boundary, modality=modality, out_gate=out_gate, norm_gain=norm_gain)


exact_mode = lax.Precision.HIGHEST
norm_eps = 1e-06

def product(left_side, right_side):
    return jnp.matmul(left_side, right_side, precision=exact_mode)

def unit_rows(matrix):
    return matrix * lax.rsqrt(lax.optimization_barrier(jnp.sum(matrix * matrix, axis=-1, keepdims=True)) + norm_eps)

def invert_unit_lower(strict):
    length = strict.shape[-1]
    unit_mat = jnp.eye(length, dtype=jnp.float32)
    nil_power = -strict
    result = unit_mat + nil_power
    for repeat in range(1, length.bit_length() - 1):
        nil_power = product(nil_power, nil_power)
        result = product(result, unit_mat + nil_power)
    return result

def block_parts(query_block, key_block, value_block, beta_block, decay_block, mark_block):
    length = query_block.shape[-2]
    decay_sum = jnp.cumsum(decay_block, axis=-2)
    counts = jnp.cumsum(mark_block, axis=-1)
    alive_rows = (counts == 0).astype(jnp.float32)
    same_doc = (counts[..., :, None] == counts[..., None, :]).astype(jnp.float32)
    row_ids = lax.broadcasted_iota(jnp.int32, (length, length), 0)
    col_ids = lax.broadcasted_iota(jnp.int32, (length, length), 1)
    strict_low = (row_ids > col_ids).astype(jnp.float32)
    with_diag = (row_ids >= col_ids).astype(jnp.float32)
    growth = jnp.exp(decay_sum)
    key_grow = key_block * growth
    key_shrink = key_block * jnp.exp(-decay_sum)
    key_gram = jnp.einsum('...ik,...jk->...ij', key_grow, key_shrink, precision=exact_mode)
    strict = key_gram * strict_low * same_doc * beta_block[..., :, None]
    solver = invert_unit_lower(strict) * beta_block[..., None, :]
    weight_rows = product(solver, key_grow * alive_rows[..., :, None])
    pseudo_rows = product(solver, value_block)
    query_grow = query_block * growth
    mixing = jnp.einsum('...ik,...jk->...ij', query_grow, key_shrink, precision=exact_mode) * with_diag * same_doc
    query_live = query_grow * alive_rows[..., :, None]
    last_sum = decay_sum[..., -1:, :]
    key_tail = key_block * jnp.exp(last_sum - decay_sum) * same_doc[..., -1, :][..., :, None]
    carry_decay = jnp.exp(last_sum[..., 0, :]) * alive_rows[..., -1:]
    return (weight_rows, pseudo_rows, mixing, query_live, key_tail, carry_decay)

def reference(query_rows, key_rows, value_rows, beta_raw, gate_latent, gate_up, dt_bias, decay_log, boundary, modality, out_gate, norm_gain):
    seq_count, length, columns = query_rows.shape
    gate_pre = jnp.dot(gate_latent.reshape(-1, RANK), gate_up, preferred_element_type=jnp.float32)
    gate_pre = gate_pre.astype(jnp.bfloat16).reshape(seq_count, length, columns)
    gate_bias = jnp.where(modality[..., None] == 1, dt_bias[1], dt_bias[0])
    rate_scale = jnp.repeat(jnp.exp(decay_log), DK)
    log_decay = -rate_scale * jax.nn.softplus(gate_pre.astype(jnp.float32) + gate_bias)
    unit_query = unit_rows(query_rows.astype(jnp.float32).reshape(seq_count, length, H, DK)) * DK ** (-0.5)
    unit_key = unit_rows(key_rows.astype(jnp.float32).reshape(seq_count, length, H, DK))
    value_wide = value_rows.astype(jnp.float32).reshape(seq_count, length, H, DK)
    beta_gate = jax.nn.sigmoid(beta_raw.astype(jnp.float32))
    blocks = length // BLOCK

    def to_blocks(tensor):
        return tensor.reshape(seq_count, blocks, BLOCK, H, DK).transpose(1, 0, 3, 2, 4)
    beta_blocks = beta_gate.reshape(seq_count, blocks, BLOCK, H).transpose(1, 0, 3, 2)
    mark_blocks = jnp.broadcast_to(boundary.reshape(seq_count, blocks, 1, BLOCK).transpose(1, 0, 2, 3), (blocks, seq_count, H, BLOCK))

    def advance(carried, inputs):
        weight_rows, pseudo_rows, mixing, query_live, key_tail, carry_decay = block_parts(*inputs)
        fresh_rows = pseudo_rows - product(weight_rows, carried)
        core_out = product(query_live, carried) + product(mixing, fresh_rows)
        carried = carry_decay[..., :, None] * carried + jnp.einsum('...ck,...cv->...kv', key_tail, fresh_rows, precision=exact_mode)
        return (carried, core_out)
    zero_state = jnp.zeros((seq_count, H, DK, DK), jnp.float32)
    finish, cores = lax.scan(advance, zero_state, (to_blocks(unit_query), to_blocks(unit_key), to_blocks(value_wide), beta_blocks, to_blocks(log_decay.reshape(seq_count, length, H, DK)), mark_blocks))
    core_out = cores.transpose(1, 0, 3, 2, 4).reshape(seq_count, length, columns).astype(jnp.bfloat16)
    core_wide = core_out.astype(jnp.float32).reshape(seq_count, length, H, DK)
    normed = core_wide * lax.rsqrt(lax.optimization_barrier(jnp.mean(core_wide * core_wide, axis=-1, keepdims=True)) + norm_eps)
    mixed_out = normed.reshape(seq_count, length, columns) * norm_gain * jax.nn.sigmoid(out_gate.astype(jnp.float32))
    return mixed_out.astype(jnp.bfloat16)
```

```python
import functools

import jax
import jax.numpy as jnp
from jax import lax
from jax.experimental import pallas as pl
from jax.experimental.pallas import tpu as pltpu
from jax.sharding import PartitionSpec as P

DK = 128
BLOCK = 128
norm_eps = 1e-06
f32 = jnp.float32
bf16 = jnp.bfloat16
ANY = pl.BlockSpec(memory_space=pl.ANY)
VMEM = pl.BlockSpec(memory_space=pltpu.VMEM)
SMEM = pl.BlockSpec(memory_space=pltpu.SMEM)
MISC = 48


def params():
    return pltpu.CompilerParams(vmem_limit_bytes=48 * 1024 * 1024)


def cost(flops, nbytes):
    return pl.CostEstimate(flops=int(flops), bytes_accessed=int(nbytes), transcendentals=0)


def dot(a, b, dims=((1,), (0,))):
    return lax.dot_general(
        a.astype(bf16), b.astype(bf16), (dims, ((), ())), preferred_element_type=f32
    )


def split(a):
    high = a.astype(bf16)
    return high, (a - high.astype(f32)).astype(bf16)


def dot3(a, b, dims=((1,), (0,))):
    ah, al = split(a)
    bh, bl = split(b)
    return dot(ah, bh, dims) + (dot(ah, bl, dims) + dot(al, bh, dims))


NT = ((1,), (1,))


def pack_kv_kernel(groups, batch, heads, key_ref, value_ref, latent_ref, beta_ref, mark_ref, kind_ref, *rest):
    outs, (extra, sem) = rest[:groups], rest[groups:]
    me = lax.axis_index("head")
    rows, width = key_ref.shape[1], key_ref.shape[2] // groups
    copies = []
    for k in range(groups):
        col = pl.multiple_of((me ^ k) * width, width)
        for i, ref in enumerate((key_ref, value_ref)):
            copies.append(
                pltpu.make_async_copy(
                    ref.at[batch, :, pl.ds(col, width)], outs[k].at[pl.ds(i * rows, rows)], sem.at[k, i]
                )
            )
            copies[-1].start()
    extra[...] = jnp.zeros_like(extra)
    lanes = width // 128
    step = rows // lanes
    for j in range(lanes):
        extra[0:step, j * 128 : (j + 1) * 128] = latent_ref[batch, j * step : (j + 1) * step, :]
    wide = jnp.concatenate(
        [
            beta_ref[batch].astype(f32),
            mark_ref[batch].astype(f32),
            kind_ref[batch].astype(f32),
            jnp.zeros((rows, 128 - heads - 2), f32),
        ],
        axis=1,
    )
    turned = jnp.transpose(jnp.concatenate([wide, jnp.zeros((128 - rows, 128), f32)], axis=0))
    for j in range(MISC // 16):
        at = step + 16 * (j // lanes)
        extra[at : at + 16, (j % lanes) * 128 : (j % lanes + 1) * 128] = turned[16 * j : 16 * j + 16].astype(bf16)
    for k in range(groups):
        copies.append(pltpu.make_async_copy(extra, outs[k].at[pl.ds(2 * rows, extra.shape[0])], sem.at[k, 2]))
        copies[-1].start()
    for c in copies:
        c.wait()


def pack_q_kernel(groups, batches, query_ref, *rest):
    outs, sem = rest[:groups], rest[groups]
    me = lax.axis_index("head")
    rows, width = query_ref.shape[1], query_ref.shape[2] // groups
    copies = []
    for k in range(groups):
        col = pl.multiple_of((me ^ k) * width, width)
        for b in range(batches):
            copies.append(
                pltpu.make_async_copy(
                    query_ref.at[b, :, pl.ds(col, width)], outs[k].at[pl.ds(b * rows, rows)], sem.at[k, b]
                )
            )
            copies[-1].start()
    for c in copies:
        c.wait()


def exchange(pieces, axis):
    count = len(pieces)
    return [pieces[0]] + [
        lax.ppermute(pieces[k], axis, [(i, i ^ k) for i in range(count)]) for k in range(1, count)
    ]


def state_kernel(groups, blocks, heads, tok, decay_ref, *rest):
    pieces = rest[:groups]
    up_ref, bias_ref = rest[groups : groups + 2]
    w_ref, u_ref, shrink_ref, growth_ref, opre_ref, mpre_ref, span_ref, mask_ref, alive_ref = rest[
        groups + 2 : groups + 11
    ]
    buf, up, levels, kinds, lasts, betas, gates, sem = rest[groups + 11 :]
    me = lax.axis_index("head")
    width = heads * DK
    per = BLOCK // tok
    copies = [
        pltpu.make_async_copy(pieces[k], buf.at[me ^ k], sem.at[k]) for k in range(groups)
    ]
    copies.append(
        pltpu.make_async_copy(up_ref.at[:, pl.ds(pl.multiple_of(me * width, width), width)], up, sem.at[groups])
    )
    for c in copies:
        c.start()
    row = lax.broadcasted_iota(jnp.int32, (BLOCK, BLOCK), 0)
    col = lax.broadcasted_iota(jnp.int32, (BLOCK, BLOCK), 1)
    low = (row >= col).astype(f32)
    low_b = low.astype(bf16)
    up_b = (row <= col).astype(bf16)
    strict = row > col
    size = 1
    count = 0
    while size < BLOCK:
        here = (row // size == col // size + 1) & ((row // size) % 2 == 1)
        levels[count] = here.astype(bf16)
        size *= 2
        count += 1
    for c in copies:
        c.wait()

    lanes = width // 128
    step = tok // lanes
    for n in range(blocks):
        tall = []
        for s in range(per):
            parts = []
            for j in range(MISC // 16):
                at = 2 * tok + step + 16 * (j // lanes)
                parts.append(buf[n * per + s, at : at + 16, (j % lanes) * 128 : (j % lanes + 1) * 128].astype(f32))
            parts.append(jnp.zeros((128 - MISC, 128), f32))
            tall.append(jnp.transpose(jnp.concatenate(parts, axis=0))[:tok])
        tall = jnp.concatenate(tall, axis=0)
        for h in range(heads):
            mine = jnp.sum(jnp.where(col == me * heads + h, tall, 0.0), axis=1, keepdims=True)
            betas[h * blocks + n] = jnp.broadcast_to(jax.nn.sigmoid(mine), (BLOCK, BLOCK))
        total = heads * groups
        mark = jnp.broadcast_to(tall[:, total : total + 1], (BLOCK, BLOCK))
        kind = jnp.broadcast_to(tall[:, total + 1 : total + 2], (BLOCK, BLOCK))
        own = dot(low_b, mark)
        other = dot(jnp.transpose(mark), up_b)
        same = own == other
        mask_ref[n] = jnp.where(same, low, 0.0)
        alive_ref[n] = (own == 0).astype(f32)
        lasts[n] = (own == other[:, BLOCK - 1 : BLOCK]).astype(f32)
        kinds[n] = kind
        gates[n] = jnp.concatenate(
            [
                buf[n * per + s, 2 * tok : 2 * tok + step, j * 128 : (j + 1) * 128]
                for s in range(per)
                for j in range(lanes)
            ],
            axis=0,
        )

    def one_head(h, _):
        lane = pl.multiple_of(h * DK, DK)
        at = pl.ds(lane, DK)
        bias_at = pl.ds(pl.multiple_of(me * width + h * DK, DK), DK)
        audio, text = bias_ref[0:1, bias_at], bias_ref[1:2, bias_at]
        rate = jnp.exp(jnp.full((1, DK), decay_ref[me * heads + h], f32))
        every = range(blocks)
        strict_all, rhs_all, tail_all, carry_all = [], [], [], []
        for n in every:
            gate = dot(gates[n], up[:, at]).astype(bf16).astype(f32)
            pre = gate + jnp.where(kinds[n] == 1.0, text, audio)
            soft = jnp.maximum(pre, 0.0) + jnp.log1p(jnp.exp(-jnp.abs(pre)))
            high, rest_part = split(-rate * soft)
            total = dot(low_b, high) + dot(low_b, rest_part)
            key = buf[n * per : (n + 1) * per, 0:tok, at].reshape(BLOCK, DK).astype(f32)
            value = buf[n * per : (n + 1) * per, tok : 2 * tok, at].reshape(BLOCK, DK).astype(f32)
            unit = key * lax.rsqrt(jnp.sum(key * key, axis=1, keepdims=True) + norm_eps)
            growth = jnp.exp(total)
            grown = unit * growth
            shrunk = unit * jnp.exp(-total)
            last = total[BLOCK - 1 : BLOCK]
            tail = unit * jnp.exp(last - total) * lasts[n]
            carry = jnp.exp(last) * alive_ref[n][BLOCK - 1 : BLOCK]
            beta = betas[h * blocks + n]
            growth_ref[h, n] = growth
            shrink_ref[h, n] = shrunk
            gram = dot(grown, shrunk, NT)
            strict_all.append(jnp.where(strict, gram * mask_ref[n] * beta, 0.0).astype(bf16))
            rhs_all.append(jnp.concatenate([beta * grown * alive_ref[n], beta * value], axis=1))
            tail_all.append(jnp.transpose(tail))
            carry_all.append(jnp.transpose(jnp.broadcast_to(carry, (BLOCK, DK))))
        inv = [-(strict_all[n] * levels[0]).astype(f32) for n in every]
        for level in range(1, count):
            corner = [strict_all[n] * levels[level] for n in every]
            inv_b = [inv[n].astype(bf16) for n in every]
            turn = [corner[n].astype(f32) + dot(inv_b[n], corner[n]) for n in every]
            inv = [inv[n] - turn[n] - dot(turn[n], inv_b[n]) for n in every]
        both = [rhs_all[n] + dot(inv[n], rhs_all[n]) for n in every]
        for n in every:
            w_ref[h, n] = both[n][:, :DK].astype(bf16)
            u_ref[h, n] = both[n][:, DK:]
        fade = [dot(tail_all[n], both[n][:, :DK]).astype(bf16) for n in every]
        offs = [dot3(tail_all[n], both[n][:, DK:]) for n in every]
        offset = jnp.zeros((DK, DK), f32)
        move = (row == col).astype(f32)
        for n in every:
            opre_ref[h, n] = offset
            mpre_ref[h, n] = move.astype(bf16)
            joint = dot(fade[n], jnp.concatenate([offset, move], axis=1))
            offset = carry_all[n] * offset + offs[n] - joint[:, :DK]
            move = carry_all[n] * move - joint[:, DK:]
        span_ref[h] = jnp.concatenate([offset, move], axis=1).astype(bf16)
        return 0

    lax.fori_loop(0, heads, one_head, 0)


def output_kernel(groups, blocks, tok, batch, *rest):
    pieces = rest[:groups]
    w_ref, u_ref, shrink_ref, growth_ref, opre_ref, mpre_ref, mask_ref, alive_ref, eo_ref, em_ref, in_ref = rest[
        groups : groups + 11
    ]
    outs = rest[groups + 11 : 2 * groups + 11]
    buf, obuf, sem, osem = rest[2 * groups + 11 :]
    h = pl.program_id(0)
    me = lax.axis_index("head")
    per = BLOCK // tok

    @pl.when(h == 0)
    def _():
        copies = [
            pltpu.make_async_copy(pieces[k].at[pl.ds(batch * tok, tok)], buf.at[me ^ k], sem.at[k])
            for k in range(groups)
        ]
        for c in copies:
            c.start()
        for c in copies:
            c.wait()

    at = pl.ds(pl.multiple_of(h * DK, DK), DK)
    every = range(blocks)
    start = eo_ref[0].astype(f32) + dot(em_ref[0], in_ref[0])
    states = [opre_ref[0, n] + dot(mpre_ref[0, n], start) for n in every]
    fresh = [u_ref[0, n] - dot(w_ref[0, n], states[n]) for n in every]
    for n in every:
        query = buf[n * per : (n + 1) * per, :, at].reshape(BLOCK, DK).astype(f32)
        unit = query * (lax.rsqrt(jnp.sum(query * query, axis=1, keepdims=True) + norm_eps) * DK ** (-0.5))
        grown = unit * growth_ref[0, n]
        mix = jnp.where(mask_ref[n] > 0.0, dot3(grown, shrink_ref[0, n], NT), 0.0)
        core = dot(grown * alive_ref[n], states[n]) + dot3(mix, fresh[n])
        obuf[n * per : (n + 1) * per, :, at] = core.astype(bf16).reshape(per, tok, DK)

    @pl.when(h == pl.num_programs(0) - 1)
    def _():
        copies = [pltpu.make_async_copy(obuf.at[me ^ k], outs[k], osem.at[k]) for k in range(groups)]
        for c in copies:
            c.start()
        for c in copies:
            c.wait()


def finish_kernel(groups, heads, *rest):
    pieces = rest[:groups]
    gate_ref, gain_ref = rest[groups : groups + 2]
    out_ref = rest[-1]
    me = lax.axis_index("head")
    for k in range(groups):
        for h in range(heads):
            at = pl.ds(pl.multiple_of((me ^ k) * (heads * DK) + h * DK, DK), DK)
            core = pieces[k][:, h * DK : (h + 1) * DK].astype(f32)
            normed = core * lax.rsqrt(jnp.mean(core * core, axis=1, keepdims=True) + norm_eps)
            out_ref[0, :, at] = (normed * gain_ref[:, at] * jax.nn.sigmoid(gate_ref[0, :, at].astype(f32))).astype(bf16)


def product(a, b):
    return jnp.einsum("hij,hjk->hik", a, b, preferred_element_type=f32)


def before(span):
    count = lax.axis_size("seq")
    place = lax.axis_index("seq")
    unit_mat = jnp.broadcast_to(jnp.eye(DK, dtype=bf16), span.shape[:1] + (DK, DK))
    offset, move = span[..., :DK], span[..., DK:]
    e_offset, e_move = jnp.zeros_like(offset), unit_mat
    incoming = jnp.zeros_like(offset)
    size = 1
    while size < count:
        final = 2 * size >= count
        payload = offset if final else jnp.concatenate([offset, move], axis=2)
        got = None
        for t in range(size):
            pairs = [
                (base + size - 1, base + size + t)
                for base in range(0, count, 2 * size)
                if base + size + t < count
            ]
            part = lax.ppermute(payload, "seq", pairs)
            got = part if got is None else got + part
        if final:
            incoming = got
            break
        got_offset, got_move = got[..., :DK], got[..., DK:]
        right = (place // size) % 2 == 1
        if size == 1:
            e_offset, e_move_new = got_offset, got_move
        else:
            e_offset = (e_offset.astype(f32) + product(e_move, got_offset)).astype(bf16)
            e_move_new = product(e_move, got_move).astype(bf16)
        e_move = jnp.where(right, e_move_new, e_move)
        offset = (offset.astype(f32) + product(move, got_offset)).astype(bf16)
        move = jnp.where(right, product(move, got_move).astype(bf16), move)
        size *= 2
    return e_offset, e_move, incoming


def per_device(
    query_rows,
    key_rows,
    value_rows,
    beta_raw,
    gate_latent,
    gate_up,
    dt_bias,
    decay_log,
    boundary,
    modality,
    out_gate,
    norm_gain,
):
    groups = lax.axis_size("head")
    batches, tok, columns = query_rows.shape
    total_heads = columns // DK
    heads = total_heads // groups
    width = heads * DK
    span = tok * groups
    blocks = span // BLOCK
    sds = jax.ShapeDtypeStruct
    lanes = width // 128
    step = tok // lanes
    extra_rows = step + 16 * (-(-(MISC // 16) // lanes))
    piece_rows = 2 * tok + extra_rows
    mark3, kind3 = boundary[..., None], modality[..., None]

    def pack_kv(batch):
        return pl.pallas_call(
            functools.partial(pack_kv_kernel, groups, batch, total_heads),
            out_shape=[sds((piece_rows, width), bf16)] * groups,
            in_specs=[ANY, ANY] + [VMEM] * 4,
            out_specs=[ANY] * groups,
            scratch_shapes=[pltpu.VMEM((extra_rows, width), bf16), pltpu.SemaphoreType.DMA((groups, 3))],
            compiler_params=params(),
            cost_estimate=cost(0, 4 * groups * piece_rows * width),
            name=f"pack_kv_{batch}",
        )(key_rows, value_rows, gate_latent, beta_raw, mark3, kind3)

    kv = [exchange(pack_kv(b), "head") for b in range(batches)]
    packed_q = pl.pallas_call(
        functools.partial(pack_q_kernel, groups, batches),
        out_shape=[sds((batches * tok, width), bf16)] * groups,
        in_specs=[ANY],
        out_specs=[ANY] * groups,
        scratch_shapes=[pltpu.SemaphoreType.DMA((groups, batches))],
        compiler_params=params(),
        cost_estimate=cost(0, 4 * groups * batches * tok * width),
        name="pack_q",
    )(query_rows)
    q_here = exchange(packed_q, "head")

    square = (heads, blocks, DK, DK)
    levels = BLOCK.bit_length() - 1
    back = []
    for b in range(batches):
        w, u, shrink, growth, opre, mpre, span_map, mask, alive = pl.pallas_call(
            functools.partial(state_kernel, groups, blocks, heads, tok),
            out_shape=[
                sds(square, bf16),
                sds(square, f32),
                sds(square, f32),
                sds(square, f32),
                sds(square, f32),
                sds(square, bf16),
                sds((heads, DK, 2 * DK), bf16),
                sds((blocks, BLOCK, BLOCK), f32),
                sds((blocks, BLOCK, BLOCK), f32),
            ],
            in_specs=[SMEM] + [ANY] * groups + [ANY, VMEM],
            out_specs=[VMEM] * 9,
            scratch_shapes=[
                pltpu.VMEM((groups, piece_rows, width), bf16),
                pltpu.VMEM((DK, width), bf16),
                pltpu.VMEM((levels, BLOCK, BLOCK), bf16),
                pltpu.VMEM((blocks, BLOCK, BLOCK), f32),
                pltpu.VMEM((blocks, BLOCK, BLOCK), f32),
                pltpu.VMEM((heads * blocks, BLOCK, BLOCK), f32),
                pltpu.VMEM((blocks, BLOCK, BLOCK), bf16),
                pltpu.SemaphoreType.DMA((groups + 1,)),
            ],
            compiler_params=params(),
            cost_estimate=cost(heads * blocks * 24 * 2 * 128**3 * 4, 8 * 2**20),
            name=f"state_maps_{b}",
        )(decay_log, *kv[b], gate_up, dt_bias)
        e_offset, e_move, incoming = before(span_map)
        per_head = pl.BlockSpec((1, blocks, DK, DK), lambda h: (h, 0, 0, 0))
        whole = pl.BlockSpec((blocks, BLOCK, BLOCK), lambda h: (0, 0, 0))
        one = pl.BlockSpec((1, DK, DK), lambda h: (h, 0, 0))
        outs = pl.pallas_call(
            functools.partial(output_kernel, groups, blocks, tok, b),
            grid=(heads,),
            out_shape=[sds((tok, width), bf16)] * groups,
            in_specs=[ANY] * groups + [per_head] * 6 + [whole] * 2 + [one] * 3,
            out_specs=[ANY] * groups,
            scratch_shapes=[
                pltpu.VMEM((groups, tok, width), bf16),
                pltpu.VMEM((groups, tok, width), bf16),
                pltpu.SemaphoreType.DMA((groups,)),
                pltpu.SemaphoreType.DMA((groups,)),
            ],
            compiler_params=params(),
            cost_estimate=cost(heads * blocks * 10 * 2 * 128**3 * 4, 8 * 2**20),
            name=f"span_outputs_{b}",
        )(*q_here, w, u, shrink, growth, opre, mpre, mask, alive, e_offset, e_move, incoming)
        back.append(exchange(outs, "head"))

    mixed = None
    for b in range(batches):
        rows = pl.BlockSpec((1, tok, columns), lambda i, b=b: (b, 0, 0))
        mixed = pl.pallas_call(
            functools.partial(finish_kernel, groups, heads),
            grid=(1,),
            out_shape=sds((batches, tok, columns), bf16),
            in_specs=[pl.BlockSpec((tok, width), lambda i: (0, 0))] * groups
            + [rows, pl.BlockSpec((1, columns), lambda i: (0, 0))]
            + ([] if b == 0 else [ANY]),
            out_specs=rows,
            input_output_aliases={} if b == 0 else {groups + 2: 0},
            compiler_params=params(),
            cost_estimate=cost(20 * tok * columns, 8 * tok * columns),
            name=f"finish_{b}",
        )(*back[b], out_gate, norm_gain[None, :], *([] if b == 0 else [mixed]))
    return mixed


def solution(mesh):
    return jax.shard_map(
        per_device,
        mesh=mesh,
        in_specs=(
            P(None, ("seq", "head"), None),
            P(None, ("seq", "head"), None),
            P(None, ("seq", "head"), None),
            P(None, ("seq", "head"), None),
            P(None, ("seq", "head"), None),
            P(),
            P(),
            P(),
            P(None, ("seq", "head")),
            P(None, ("seq", "head")),
            P(None, ("seq", "head"), None),
            P(),
        ),
        out_specs=P(None, ("seq", "head"), None),
        check_vma=False,
    )
```

```python
import functools

import jax
import jax.numpy as jnp
from jax import lax
from jax.experimental import pallas as pl
from jax.experimental.pallas import tpu as pltpu
from jax.sharding import PartitionSpec as P

DK = 128
BLOCK = 128
norm_eps = 1e-06
LOG2E = 1.4426950408889634
f32 = jnp.float32
bf16 = jnp.bfloat16
ANY = pl.BlockSpec(memory_space=pl.ANY)
VMEM = pl.BlockSpec(memory_space=pltpu.VMEM)
SMEM = pl.BlockSpec(memory_space=pltpu.SMEM)


def params(mib=48):
    return pltpu.CompilerParams(vmem_limit_bytes=mib * 1024 * 1024)


def misc_rows(total_heads):
    return -(-(total_heads + 2) // 16) * 16


def cost(flops, nbytes):
    return pl.CostEstimate(flops=int(flops), bytes_accessed=int(nbytes), transcendentals=0)


def dot(a, b, dims=((1,), (0,))):
    return lax.dot_general(
        a.astype(bf16), b.astype(bf16), (dims, ((), ())), preferred_element_type=f32
    )


def split(a):
    high = a.astype(bf16)
    return high, (a - high.astype(f32)).astype(bf16)


def dot3(a, b, dims=((1,), (0,))):
    ah, al = split(a)
    bh, bl = split(b)
    return dot(ah, bh, dims) + (dot(ah, bl, dims) + dot(al, bh, dims))


NT = ((1,), (1,))


def pack_kv_kernel(sub, batch, heads, key_ref, value_ref, latent_ref, beta_ref, mark_ref, kind_ref, *rest):
    outs, (extra, sem) = rest[:sub], rest[sub:]
    lo = lax.rem(lax.axis_index("head"), sub)
    rows, width = key_ref.shape[1], key_ref.shape[2] // sub
    copies = []
    for k in range(sub):
        col = pl.multiple_of((lo ^ k) * width, width)
        for i, ref in enumerate((key_ref, value_ref)):
            copies.append(
                pltpu.make_async_copy(
                    ref.at[batch, :, pl.ds(col, width)], outs[k].at[pl.ds(i * rows, rows)], sem.at[k, i]
                )
            )
            copies[-1].start()
    extra[...] = jnp.zeros_like(extra)
    lanes = width // 128
    wide = jnp.concatenate(
        [
            beta_ref[batch].astype(f32),
            mark_ref[batch].astype(f32),
            kind_ref[batch].astype(f32),
            jnp.zeros((rows, 128 - heads - 2), f32),
        ],
        axis=1,
    )
    turned = jnp.transpose(jnp.concatenate([wide, jnp.zeros((128 - rows, 128), f32)], axis=0)).astype(bf16)
    chunks = [latent_ref[batch, 16 * j : 16 * j + 16] for j in range(rows // 16)]
    chunks += [turned[16 * j : 16 * j + 16] for j in range(misc_rows(heads) // 16)]
    for c, chunk in enumerate(chunks):
        extra[16 * (c // lanes) : 16 * (c // lanes) + 16, (c % lanes) * 128 : (c % lanes + 1) * 128] = chunk
    for k in range(sub):
        copies.append(pltpu.make_async_copy(extra, outs[k].at[pl.ds(2 * rows, extra.shape[0])], sem.at[k, 2]))
        copies[-1].start()
    for c in copies:
        c.wait()


def pack_q_kernel(sub, batches, query_ref, *rest):
    outs, sem = rest[-sub - 1 : -1], rest[-1]
    lo = lax.rem(lax.axis_index("head"), sub)
    rows, width = query_ref.shape[1], query_ref.shape[2] // sub
    copies = []
    for k in range(sub):
        col = pl.multiple_of((lo ^ k) * width, width)
        for b in range(batches):
            copies.append(
                pltpu.make_async_copy(
                    query_ref.at[b, :, pl.ds(col, width)], outs[k].at[pl.ds(b * rows, rows)], sem.at[k, b]
                )
            )
            copies[-1].start()
    for c in copies:
        c.wait()


def exchange(pieces):
    count = lax.axis_size("head")
    got = {
        k: lax.ppermute(pieces[k], "head", [(i, i ^ k) for i in range(count)]) for k in range(len(pieces) - 1, 0, -1)
    }
    return [pieces[0]] + [got[k] for k in range(1, len(pieces))]


def state_kernel(sub, outer, blocks, heads, tok, hp, decay_ref, *rest):
    pieces = rest[:sub]
    up_ref, bias_ref = rest[sub : sub + 2]
    w_ref, u_ref, shrink_ref, growth_ref, opre_ref, mpre_ref, mask_ref, alive_ref = rest[sub + 2 : sub + 10]
    parts = rest[sub + 10 : sub + 10 + outer]
    buf, up, levels, kinds, lasts, betas, gates, spans, sem, part_sem = rest[sub + 10 + outer :]
    me = lax.rem(lax.axis_index("head"), sub)
    hi = lax.div(lax.axis_index("head"), sub)
    total_heads = heads * sub
    width = heads * DK
    per = BLOCK // tok
    row = lax.broadcasted_iota(jnp.int32, (BLOCK, BLOCK), 0)
    col = lax.broadcasted_iota(jnp.int32, (BLOCK, BLOCK), 1)
    low = (row >= col).astype(f32)
    low_b = low.astype(bf16)
    up_b = (row <= col).astype(bf16)
    unit_mat = (row == col).astype(bf16)
    count = BLOCK.bit_length() - 1
    step = pl.program_id(0)

    @pl.when(step == 0)
    def _():
        copies = [pltpu.make_async_copy(pieces[k], buf.at[me ^ k], sem.at[k]) for k in range(sub)]
        copies.append(
            pltpu.make_async_copy(up_ref.at[:, pl.ds(pl.multiple_of(me * width, width), width)], up, sem.at[sub])
        )
        for c in copies:
            c.start()
        for level in range(count):
            size = 2**level
            here = (row // size == col // size + 1) & ((row // size) % 2 == 1)
            levels[level] = here.astype(bf16)
        for c in copies:
            c.wait()
        lanes = width // 128
        misc = misc_rows(total_heads)

        def chunk(source, c):
            at = 2 * tok + 16 * (c // lanes)
            return buf[source, at : at + 16, (c % lanes) * 128 : (c % lanes + 1) * 128]

        for n in range(blocks):
            tall = []
            for s in range(n * per, (n + 1) * per):
                values = [chunk(s, tok // 16 + j).astype(f32) for j in range(misc // 16)]
                values.append(jnp.zeros((128 - misc, 128), f32))
                tall.append(jnp.transpose(jnp.concatenate(values, axis=0))[:tok])
            tall = jnp.concatenate(tall, axis=0)
            sig = jax.nn.sigmoid(tall)
            for h in range(heads):
                mine = jnp.sum(jnp.where(col == me * heads + h, sig, 0.0), axis=1, keepdims=True)
                betas[h, n] = jnp.broadcast_to(mine, (BLOCK, BLOCK))
            mark = jnp.broadcast_to(tall[:, total_heads : total_heads + 1], (BLOCK, BLOCK))
            own = dot(low_b, mark)
            other = dot(jnp.transpose(mark), up_b)
            mask_ref[n] = jnp.where(own == other, low, 0.0)
            alive_ref[n] = (own == 0).astype(f32)
            lasts[n] = (own == other[:, BLOCK - 1 : BLOCK]).astype(f32)
            kinds[n] = jnp.broadcast_to(tall[:, total_heads + 1 : total_heads + 2], (BLOCK, BLOCK))
            gates[n] = jnp.concatenate(
                [chunk(s, j) for s in range(n * per, (n + 1) * per) for j in range(tok // 16)], axis=0
            )

    low2 = jnp.concatenate([low_b, low_b], axis=1)
    lower = (row > col).astype(f32)
    items = [(i, n) for i in range(hp) for n in range(blocks)]
    strict_all, rhs_all, tail_all, carry_all = {}, {}, {}, {}
    for i in range(hp):
        h = step * hp + i
        at = pl.ds(pl.multiple_of(h * DK, DK), DK)
        bias_at = pl.ds(pl.multiple_of(me * width + h * DK, DK), DK)
        audio, text = bias_ref[0:1, bias_at], bias_ref[1:2, bias_at]
        rate = -LOG2E * jnp.exp(jnp.full((1, DK), decay_ref[me * heads + h], f32))
        for n in range(blocks):
            gate = dot(gates[n], up[:, at]).astype(bf16).astype(f32)
            pre = gate + jnp.where(kinds[n] == 1.0, text, audio)
            soft = jnp.maximum(pre, 0.0) + jnp.log(1.0 + jnp.exp(-jnp.abs(pre)))
            high, rest_part = split(rate * soft)
            total = dot(low2, jnp.concatenate([high, rest_part], axis=0))
            key = buf[n * per : (n + 1) * per, 0:tok, at].reshape(BLOCK, DK).astype(f32)
            value = buf[n * per : (n + 1) * per, tok : 2 * tok, at].reshape(BLOCK, DK).astype(f32)
            unit = key * lax.rsqrt(jnp.sum(key * key, axis=1, keepdims=True) + norm_eps)
            growth = jnp.exp2(total)
            grown = unit * growth
            shrunk, shrunk_rest = split(unit * jnp.exp2(-total))
            last = total[BLOCK - 1 : BLOCK]
            tail = unit * (jnp.exp2(last - total) * lasts[n])
            carry = jnp.exp2(last) * alive_ref[n, BLOCK - 1 : BLOCK]
            beta = betas[h, n]
            growth_ref[i, n] = growth
            shrink_ref[i, n, :, :DK] = shrunk
            shrink_ref[i, n, :, DK:] = shrunk_rest
            gram = dot(grown, shrunk, NT)
            strict_all[i, n] = (gram * (mask_ref[n] * lower) * beta).astype(bf16)
            rhs_all[i, n] = jnp.concatenate([beta * grown * alive_ref[n], beta * value], axis=1)
            tail_all[i, n] = jnp.transpose(tail)
            carry_all[i, n] = carry
    turned = jnp.transpose(jnp.concatenate([carry_all[t] for t in items] + [jnp.zeros((BLOCK - len(items), DK), f32)]))
    carry_all = {t: turned[:, j : j + 1] for j, t in enumerate(items)}
    inv = {t: unit_mat - strict_all[t] * levels[0] for t in items}
    for level in range(1, count):
        size = 2**level
        corner = {t: strict_all[t] * levels[level] for t in items}
        if size < 16:
            turn = {t: dot(inv[t], corner[t]) for t in items}
            inv = {t: inv[t] - dot(turn[t], inv[t]).astype(bf16) for t in items}
        else:
            pairs = BLOCK // (2 * size)
            four = {t: inv[t].reshape(pairs, 2, size, BLOCK) for t in items}
            odd = {t: four[t][:, 1].reshape(BLOCK // 2, BLOCK) for t in items}
            turn = {t: dot(odd[t], corner[t]) for t in items}
            odd = {t: odd[t] - dot(turn[t], inv[t]).astype(bf16) for t in items}
            inv = {
                t: jnp.stack([four[t][:, 0], odd[t].reshape(pairs, size, BLOCK)], axis=1).reshape(BLOCK, BLOCK)
                for t in items
            }
    both = {t: rhs_all[t] + dot(inv[t] - unit_mat, rhs_all[t]) for t in items}
    fade, offs = {}, {}
    for t in items:
        i, n = t
        w = both[t][:, :DK].astype(bf16)
        w_ref[i, n] = w
        u_ref[i, n] = both[t][:, DK:]
        uh, ul = split(both[t][:, DK:])
        th, tl = split(tail_all[t])
        joint = dot(th, jnp.concatenate([w, uh], axis=1))
        fade[t] = joint[:, :DK]
        offs[t] = joint[:, DK:] + dot(jnp.concatenate([th, tl], axis=1), jnp.concatenate([ul, uh], axis=0))
    offset = {i: offs[i, 0] for i in range(hp)}
    move = {i: jnp.where(row == col, carry_all[i, 0], 0.0) - fade[i, 0] for i in range(hp)}
    for n in range(1, blocks):
        for i in range(hp):
            opre_ref[i, n - 1] = offset[i]
            mpre_ref[i, n - 1] = move[i].astype(bf16)
            joint = dot(fade[i, n], jnp.concatenate([offset[i], move[i]], axis=1))
            offset[i] = carry_all[i, n] * offset[i] + offs[i, n] - joint[:, :DK]
            move[i] = carry_all[i, n] * move[i] - joint[:, DK:]
    for i in range(hp):
        spans[step * hp + i] = jnp.concatenate([offset[i], move[i]], axis=1).astype(bf16)

    @pl.when(step == pl.num_programs(0) - 1)
    def _():
        share = heads // outer
        copies = [
            pltpu.make_async_copy(spans.at[pl.ds((hi ^ j) * share, share)], parts[j], part_sem.at[j])
            for j in range(outer)
        ]
        for c in copies:
            c.start()
        for c in copies:
            c.wait()


def joined(later, earlier):
    both = dot(later[1], jnp.concatenate([earlier[0], earlier[1]], axis=1))
    return (later[0].astype(f32) + both[:, :DK]).astype(bf16), both[:, DK:].astype(bf16)


def ordered(outer, parts, order):
    hi = lax.div(lax.axis_index("head"), lax.axis_size("head") // outer)
    for j in range(outer):
        order[hi ^ j] = parts[j][...]


def compose_kernel(outer, share, *rest):
    parts, out_ref, order = rest[:outer], rest[outer], rest[outer + 1]
    ordered(outer, parts, order)
    for h in range(share):
        whole = (order[0, h, :, :DK], order[0, h, :, DK:])
        for o in range(1, outer):
            whole = joined((order[o, h, :, :DK], order[o, h, :, DK:]), whole)
        out_ref[h, :, :DK] = whole[0]
        out_ref[h, :, DK:] = whole[1]


def seed_kernel(outer, share, raw, *rest):
    parts = rest[:outer]
    early_ref, in_ref = rest[outer : outer + 2]
    outs = rest[outer + 2 : 2 * outer + 2]
    order, seeds = rest[2 * outer + 2 :]
    hi = lax.div(lax.axis_index("head"), lax.axis_size("head") // outer)
    ordered(outer, parts, order)
    row = lax.broadcasted_iota(jnp.int32, (DK, DK), 0)
    col = lax.broadcasted_iota(jnp.int32, (DK, DK), 1)
    odd = lax.rem(lax.axis_index("seq"), 2) == 1
    for h in range(share):
        incoming = in_ref[h]
        through = dot(early_ref[h, :, DK:], incoming)
        if raw:
            through = jnp.where(odd, through, incoming.astype(f32))
        state = (early_ref[h, :, :DK].astype(f32) + through).astype(bf16)
        seeds[0, h] = state
        for o in range(1, outer):
            moved = dot(order[o - 1, h, :, DK:], state)
            state = (order[o - 1, h, :, :DK].astype(f32) + moved).astype(bf16)
            seeds[o, h] = state
    for j in range(outer):
        outs[j][...] = seeds[hi ^ j]


def output_kernel(sub, outer, blocks, heads, tok, batch, hp, *rest):
    pieces = rest[:sub]
    w_ref, u_ref, shrink_ref, growth_ref, opre_ref, mpre_ref, mask_ref, alive_ref = rest[sub : sub + 8]
    seeds = rest[sub + 8 : sub + 8 + outer]
    outs = rest[sub + 8 + outer : 2 * sub + 8 + outer]
    buf, obuf, begin, sem, osem, seed_sem = rest[2 * sub + 8 + outer :]
    step = pl.program_id(0)
    lo = lax.rem(lax.axis_index("head"), sub)
    hi = lax.div(lax.axis_index("head"), sub)
    per = BLOCK // tok

    @pl.when(step == 0)
    def _():
        share = heads // outer
        copies = [
            pltpu.make_async_copy(pieces[k].at[pl.ds(batch * tok, tok)], buf.at[lo ^ k], sem.at[k])
            for k in range(sub)
        ]
        copies += [
            pltpu.make_async_copy(seeds[j], begin.at[pl.ds((hi ^ j) * share, share)], seed_sem.at[j])
            for j in range(outer)
        ]
        for c in copies:
            c.start()
        for c in copies:
            c.wait()

    items = [(i, n) for i in range(hp) for n in range(blocks)]
    at = [pl.ds(pl.multiple_of((step * hp + i) * DK, DK), DK) for i in range(hp)]
    start = [begin[step * hp + i].astype(f32) for i in range(hp)]
    states = {
        (i, n): start[i] if n == 0 else opre_ref[i, n - 1] + dot(mpre_ref[i, n - 1], start[i]) for i, n in items
    }
    grown, mix = {}, {}
    for i, n in items:
        query = buf[n * per : (n + 1) * per, :, at[i]].reshape(BLOCK, DK).astype(f32)
        unit = query * (lax.rsqrt(jnp.sum(query * query, axis=1, keepdims=True) + norm_eps) * DK ** (-0.5))
        grown[i, n] = unit * growth_ref[i, n]
        gh, gl = split(grown[i, n])
        shrunk = shrink_ref[i, n]
        mix[i, n] = mask_ref[n] * dot(
            jnp.concatenate([gh, gh, gl], axis=1), jnp.concatenate([shrunk, shrunk[:, :DK]], axis=1), NT
        )
    fresh = {(i, n): u_ref[i, n] - dot(w_ref[i, n], states[i, n]) for i, n in items}
    for i, n in items:
        fh, fl = split(fresh[i, n])
        mh, ml = split(mix[i, n])
        live = (grown[i, n] * alive_ref[n]).astype(bf16)
        core = dot(
            jnp.concatenate([live, mh, mh, ml], axis=1),
            jnp.concatenate([states[i, n].astype(bf16), fh, fl, fh], axis=0),
        )
        obuf[n * per : (n + 1) * per, :, at[i]] = core.astype(bf16).reshape(per, tok, DK)

    @pl.when(step == pl.num_programs(0) - 1)
    def _():
        copies = [pltpu.make_async_copy(obuf.at[lo ^ k], outs[k], osem.at[k]) for k in range(sub)]
        for c in copies:
            c.start()
        for c in copies:
            c.wait()


def finish_kernel(sub, heads, *rest):
    pieces = rest[:sub]
    gate_ref, gain_ref = rest[sub : sub + 2]
    out_ref = rest[-1]
    me = lax.rem(lax.axis_index("head"), sub)
    for k in range(sub):
        for h in range(heads):
            at = pl.ds(pl.multiple_of((me ^ k) * (heads * DK) + h * DK, DK), DK)
            core = pieces[k][:, h * DK : (h + 1) * DK].astype(f32)
            normed = core * lax.rsqrt(jnp.mean(core * core, axis=1, keepdims=True) + norm_eps)
            out_ref[0, :, at] = (normed * gain_ref[:, at] * jax.nn.sigmoid(gate_ref[0, :, at].astype(f32))).astype(bf16)


def product(a, b):
    return jnp.einsum("hij,hjk->hik", a, b, preferred_element_type=f32)


def before(span):
    count = lax.axis_size("seq")
    place = lax.axis_index("seq")
    unit_mat = jnp.broadcast_to(jnp.eye(DK, dtype=bf16), span.shape[:1] + (DK, DK))
    raw = True
    early, whole = None, span
    size = 1
    while size < count:
        final = 2 * size >= count
        payload = whole[..., :DK] if final else whole
        got = None
        for t in range(size):
            pairs = [
                (base + size - 1, base + size + t)
                for base in range(0, count, 2 * size)
                if base + size + t < count
            ]
            part = lax.ppermute(payload, "seq", pairs)
            got = part if got is None else got + part
        if final:
            break
        right = (place // size) % 2 == 1
        if size == 1:
            early = got
        else:
            e_move = early[..., DK:]
            if raw:
                e_move = jnp.where(place % 2 == 1, e_move, unit_mat)
            raw = False
            moved = product(e_move, got)
            early = jnp.concatenate(
                [
                    (early[..., :DK].astype(f32) + moved[..., :DK]).astype(bf16),
                    jnp.where(right, moved[..., DK:].astype(bf16), e_move),
                ],
                axis=2,
            )
        moved = product(whole[..., DK:], got)
        whole = jnp.concatenate(
            [
                (whole[..., :DK].astype(f32) + moved[..., :DK]).astype(bf16),
                jnp.where(right, moved[..., DK:].astype(bf16), whole[..., DK:]),
            ],
            axis=2,
        )
        size *= 2
    if early is None:
        early = jnp.concatenate([jnp.zeros_like(unit_mat), unit_mat], axis=2)
    return early, got, raw


def per_device(
    query_rows,
    key_rows,
    value_rows,
    beta_raw,
    gate_latent,
    gate_up,
    dt_bias,
    decay_log,
    boundary,
    modality,
    out_gate,
    norm_gain,
):
    places = lax.axis_size("head")
    batches, tok, columns = query_rows.shape
    sub = min(places, 4)
    outer = places // sub
    total_heads = columns // DK
    heads = total_heads // sub
    share = heads // outer
    width = heads * DK
    blocks = tok * sub // BLOCK
    sds = jax.ShapeDtypeStruct
    extra_rows = 16 * -(-(tok // 16 + misc_rows(total_heads) // 16) // (width // 128))
    piece_rows = 2 * tok + extra_rows
    mark3, kind3 = boundary[..., None], modality[..., None]

    def pack_kv(batch):
        return pl.pallas_call(
            functools.partial(pack_kv_kernel, sub, batch, total_heads),
            out_shape=[sds((piece_rows, width), bf16)] * sub,
            in_specs=[ANY, ANY] + [VMEM] * 4,
            out_specs=[ANY] * sub,
            scratch_shapes=[pltpu.VMEM((extra_rows, width), bf16), pltpu.SemaphoreType.DMA((sub, 3))],
            compiler_params=params(),
            cost_estimate=cost(0, 4 * sub * piece_rows * width),
            name=f"pack_kv_{batch}",
        )(key_rows, value_rows, gate_latent, beta_raw, mark3, kind3)

    kv = [exchange(pack_kv(b)) for b in range(batches)]
    hp = max(1, 8 // blocks)
    while heads % hp:
        hp -= 1
    before_rows = max(1, blocks - 1)

    def by_head(*dims):
        return pl.BlockSpec((hp, *dims), lambda i: (i,) + (0,) * len(dims))

    per_head = by_head(blocks, DK, DK)
    wide_head = by_head(blocks, DK, 2 * DK)
    pre_head = by_head(before_rows, DK, DK)
    whole = pl.BlockSpec((blocks, BLOCK, BLOCK), lambda i: (0, 0, 0))
    square = (heads, blocks, DK, DK)
    levels = BLOCK.bit_length() - 1
    local, seeds = [], []
    q_here = None
    for b in range(batches):
        made = pl.pallas_call(
            functools.partial(state_kernel, sub, outer, blocks, heads, tok, hp),
            grid=(heads // hp,),
            out_shape=[
                sds(square, bf16),
                sds(square, f32),
                sds((heads, blocks, DK, 2 * DK), bf16),
                sds(square, f32),
                sds((heads, before_rows, DK, DK), f32),
                sds((heads, before_rows, DK, DK), bf16),
                sds((blocks, BLOCK, BLOCK), f32),
                sds((blocks, BLOCK, BLOCK), f32),
            ]
            + [sds((share, DK, 2 * DK), bf16)] * outer,
            in_specs=[SMEM] + [ANY] * sub + [ANY, VMEM],
            out_specs=[per_head, per_head, wide_head, per_head, pre_head, pre_head, whole, whole] + [ANY] * outer,
            scratch_shapes=[
                pltpu.VMEM((sub, piece_rows, width), bf16),
                pltpu.VMEM((DK, width), bf16),
                pltpu.VMEM((levels, BLOCK, BLOCK), bf16),
                pltpu.VMEM((blocks, BLOCK, BLOCK), f32),
                pltpu.VMEM((blocks, BLOCK, BLOCK), f32),
                pltpu.VMEM((heads, blocks, BLOCK, BLOCK), f32),
                pltpu.VMEM((blocks, BLOCK, BLOCK), bf16),
                pltpu.VMEM((heads, DK, 2 * DK), bf16),
                pltpu.SemaphoreType.DMA((sub + 1,)),
                pltpu.SemaphoreType.DMA((outer,)),
            ],
            compiler_params=params(),
            cost_estimate=cost(heads * blocks * 24 * 2 * 128**3 * 4, 8 * 2**20),
            name=f"state_maps_{b}",
        )(decay_log, *kv[b], gate_up, dt_bias)
        local.append(made[:8])
        if q_here is None:
            q_here = exchange(
                pl.pallas_call(
                    functools.partial(pack_q_kernel, sub, batches),
                    out_shape=[sds((batches * tok, width), bf16)] * sub,
                    in_specs=[ANY, ANY],
                    out_specs=[ANY] * sub,
                    scratch_shapes=[pltpu.SemaphoreType.DMA((sub, batches))],
                    compiler_params=params(),
                    cost_estimate=cost(0, 4 * sub * batches * tok * width),
                    name="pack_q",
                )(query_rows, made[-1])
            )
        count = lax.axis_size("head")

        def swap(parts):
            return [parts[0]] + [
                lax.ppermute(parts[j], "head", [(i, i ^ (j * sub)) for i in range(count)]) for j in range(1, outer)
            ]

        parts = swap(made[8:])
        total = pl.pallas_call(
            functools.partial(compose_kernel, outer, share),
            out_shape=sds((share, DK, 2 * DK), bf16),
            in_specs=[VMEM] * outer,
            out_specs=VMEM,
            scratch_shapes=[pltpu.VMEM((outer, share, DK, 2 * DK), bf16)],
            compiler_params=params(),
            cost_estimate=cost(share * outer * 4 * 128**3, 2**20),
            name=f"compose_{b}",
        )(*parts)
        early, incoming, raw = before(total)
        mine = pl.pallas_call(
            functools.partial(seed_kernel, outer, share, raw),
            out_shape=[sds((share, DK, DK), bf16)] * outer,
            in_specs=[VMEM] * (outer + 2),
            out_specs=[VMEM] * outer,
            scratch_shapes=[
                pltpu.VMEM((outer, share, DK, 2 * DK), bf16),
                pltpu.VMEM((outer, share, DK, DK), bf16),
            ],
            compiler_params=params(),
            cost_estimate=cost(share * outer * 4 * 128**3, 2**20),
            name=f"seeds_{b}",
        )(*parts, early, incoming)
        seeds.append(swap(mine))
    back = []
    for b in range(batches):
        outs = pl.pallas_call(
            functools.partial(output_kernel, sub, outer, blocks, heads, tok, b, hp),
            grid=(heads // hp,),
            out_shape=[sds((tok, width), bf16)] * sub,
            in_specs=[ANY] * sub
            + [per_head, per_head, wide_head, per_head, pre_head, pre_head]
            + [whole] * 2
            + [ANY] * outer,
            out_specs=[ANY] * sub,
            scratch_shapes=[
                pltpu.VMEM((sub, tok, width), bf16),
                pltpu.VMEM((sub, tok, width), bf16),
                pltpu.VMEM((heads, DK, DK), bf16),
                pltpu.SemaphoreType.DMA((sub,)),
                pltpu.SemaphoreType.DMA((sub,)),
                pltpu.SemaphoreType.DMA((outer,)),
            ],
            compiler_params=params(),
            cost_estimate=cost(heads * blocks * 10 * 2 * 128**3 * 4, 8 * 2**20),
            name=f"span_outputs_{b}",
        )(*q_here, *local[b], *seeds[b])
        back.append(exchange(outs))

    mixed = None
    for b in range(batches):
        rows = pl.BlockSpec((1, tok, columns), lambda i, b=b: (b, 0, 0))
        mixed = pl.pallas_call(
            functools.partial(finish_kernel, sub, heads),
            grid=(1,),
            out_shape=sds((batches, tok, columns), bf16),
            in_specs=[pl.BlockSpec((tok, width), lambda i: (0, 0))] * sub
            + [rows, pl.BlockSpec((1, columns), lambda i: (0, 0))]
            + ([] if b == 0 else [ANY]),
            out_specs=rows,
            input_output_aliases={} if b == 0 else {sub + 2: 0},
            compiler_params=params(),
            cost_estimate=cost(20 * tok * columns, 8 * tok * columns),
            name=f"finish_{b}",
        )(*back[b], out_gate, norm_gain[None, :], *([] if b == 0 else [mixed]))
    return mixed


def solution(mesh):
    return jax.shard_map(
        per_device,
        mesh=mesh,
        in_specs=(
            P(None, ("seq", "head"), None),
            P(None, ("seq", "head"), None),
            P(None, ("seq", "head"), None),
            P(None, ("seq", "head"), None),
            P(None, ("seq", "head"), None),
            P(),
            P(),
            P(),
            P(None, ("seq", "head")),
            P(None, ("seq", "head")),
            P(None, ("seq", "head"), None),
            P(),
        ),
        out_specs=P(None, ("seq", "head"), None),
        check_vma=False,
    )
```

```python
import functools

import jax
import jax.numpy as jnp
from jax import lax
from jax.experimental import pallas as pl
from jax.experimental.pallas import tpu as pltpu
from jax.sharding import PartitionSpec as P

DK = 128
BLOCK = 128
norm_eps = 1e-06
LOG2E = 1.4426950408889634
f32 = jnp.float32
bf16 = jnp.bfloat16
ANY = pl.BlockSpec(memory_space=pl.ANY)
VMEM = pl.BlockSpec(memory_space=pltpu.VMEM)
SMEM = pl.BlockSpec(memory_space=pltpu.SMEM)
PACK_MIB = 48
SCALE = 0.1


def params(mib=48):
    return pltpu.CompilerParams(vmem_limit_bytes=mib * 1024 * 1024)


def misc_rows(heads):
    return -(-(heads + 2) // 16) * 16


def cost(flops, nbytes):
    return pl.CostEstimate(flops=int(flops), bytes_accessed=int(nbytes), transcendentals=0)


def dot(a, b, dims=((1,), (0,))):
    return lax.dot_general(
        a.astype(bf16), b.astype(bf16), (dims, ((), ())), preferred_element_type=f32
    )


def split(a):
    high = a.astype(bf16)
    return high, (a - high.astype(f32)).astype(bf16)


def dot3(a, b, dims=((1,), (0,))):
    ah, al = split(a)
    bh, bl = split(b)
    return dot(ah, bh, dims) + (dot(ah, bl, dims) + dot(al, bh, dims))


NT = ((1,), (1,))


def pack_kv_kernel(sub, batch, heads, key_ref, value_ref, latent_ref, beta_ref, mark_ref, kind_ref, *rest):
    outs, (latent, beta, mark, kind, turned, sem, small_sem) = rest[-sub - 7 : -7], rest[-7:]
    lo = lax.rem(lax.axis_index("head"), sub)
    rows, width = key_ref.shape[1], key_ref.shape[2] // sub
    small = [
        pltpu.make_async_copy(source, target, small_sem.at[i])
        for i, (source, target) in enumerate(
            ((latent_ref.at[batch], latent), (beta_ref.at[batch], beta), (mark_ref, mark), (kind_ref, kind))
        )
    ]
    for c in small:
        c.start()
    copies = []
    for k in range(sub):
        col = pl.multiple_of((lo ^ k) * width, width)
        for i, ref in enumerate((key_ref, value_ref)):
            copies.append(
                pltpu.make_async_copy(
                    ref.at[batch, :, pl.ds(col, width)], outs[k].at[pl.ds(i * rows, rows)], sem.at[k, i]
                )
            )
            copies[-1].start()
    for c in small:
        c.wait()
    lanes = width // 128
    total = beta.shape[1]
    misc = misc_rows(heads)
    wide = jnp.concatenate([beta[...].astype(f32), jnp.zeros((rows, 128 - total), f32)], axis=1)
    turned[...] = jnp.transpose(jnp.concatenate([wide, jnp.zeros((128 - rows, 128), f32)], axis=0))
    tokens = jnp.concatenate([mark[batch : batch + 1].astype(f32), kind[batch : batch + 1].astype(f32)], axis=0)
    tokens = jnp.concatenate([tokens, jnp.zeros((2, 128 - rows), f32)], axis=1)
    for k in range(sub):
        own = turned[pl.ds(pl.multiple_of((lo ^ k) * heads, heads), heads), :]
        values = jnp.concatenate([own, tokens, jnp.zeros((misc - heads - 2, 128), f32)], axis=0).astype(bf16)
        chunks = [latent[16 * j : 16 * j + 16] for j in range(rows // 16)]
        chunks += [values[16 * j : 16 * j + 16] for j in range(misc // 16)]
        chunks += [jnp.zeros((16, 128), bf16)] * (-len(chunks) % lanes)
        for c, chunk in enumerate(chunks):
            at = 2 * rows + 16 * (c // lanes)
            outs[k][at : at + 16, (c % lanes) * 128 : (c % lanes + 1) * 128] = chunk
    for c in copies:
        c.wait()


def pack_q_kernel(sub, batches, query_ref, *rest):
    outs, sem = rest[-sub - 1 : -1], rest[-1]
    lo = lax.rem(lax.axis_index("head"), sub)
    rows, width = query_ref.shape[1], query_ref.shape[2] // sub
    copies = []
    for k in range(sub):
        col = pl.multiple_of((lo ^ k) * width, width)
        for b in range(batches):
            copies.append(
                pltpu.make_async_copy(
                    query_ref.at[b, :, pl.ds(col, width)], outs[k].at[pl.ds(b * rows, rows)], sem.at[k, b]
                )
            )
            copies[-1].start()
    for c in copies:
        c.wait()


def exchange(pieces):
    count = lax.axis_size("head")
    got = {
        k: lax.ppermute(pieces[k], "head", [(i, i ^ k) for i in range(count)]) for k in range(len(pieces) - 1, 0, -1)
    }
    return [pieces[0]] + [got[k] for k in range(1, len(pieces))]


def place(outer, first, share, hp):
    at = pl.program_id(0) * hp
    hi = lax.div(lax.axis_index("head"), lax.axis_size("head") // outer)
    return (hi ^ (first + lax.div(at, share))) * share + lax.rem(at, share)


def state_kernel(sub, outer, first, blocks, heads, tok, hp, decay_ref, *rest):
    pieces = rest[:sub]
    up_ref, bias_ref = rest[sub : sub + 2]
    w_ref, u_ref, shrink_ref, growth_ref, opre_ref, mpre_ref, span_ref, mask_ref, alive_ref = rest[-17:-8]
    buf, up, levels, kinds, lasts, values, gates, sem = rest[-8:]
    me = lax.rem(lax.axis_index("head"), sub)
    start = place(outer, first, heads // outer, hp)
    width = heads * DK
    per = BLOCK // tok
    row = lax.broadcasted_iota(jnp.int32, (BLOCK, BLOCK), 0)
    col = lax.broadcasted_iota(jnp.int32, (BLOCK, BLOCK), 1)
    low = (row >= col).astype(f32)
    low_b = low.astype(bf16)
    up_b = (row <= col).astype(bf16)
    unit_mat = (row == col).astype(bf16)
    count = BLOCK.bit_length() - 1
    step = pl.program_id(0)

    @pl.when(step == 0)
    def _():
        copies = [pltpu.make_async_copy(pieces[k], buf.at[me ^ k], sem.at[k]) for k in range(sub)]
        copies.append(
            pltpu.make_async_copy(up_ref.at[:, pl.ds(pl.multiple_of(me * width, width), width)], up, sem.at[sub])
        )
        for c in copies:
            c.start()
        for level in range(count):
            size = 2**level
            here = (row // size == col // size + 1) & ((row // size) % 2 == 1)
            levels[level] = here.astype(bf16)
        for c in copies:
            c.wait()
        lanes = width // 128
        misc = misc_rows(heads)

        def chunk(source, c):
            at = 2 * tok + 16 * (c // lanes)
            return buf[source, at : at + 16, (c % lanes) * 128 : (c % lanes + 1) * 128]

        for n in range(blocks):
            tall = jnp.concatenate(
                [
                    jnp.concatenate([chunk(s, tok // 16 + j).astype(f32) for j in range(misc // 16)], axis=0)[:, :tok]
                    for s in range(n * per, (n + 1) * per)
                ],
                axis=1,
            )
            values[n] = jax.nn.sigmoid(tall)
            mark = tall[heads : heads + 1]
            two = jnp.transpose(jnp.concatenate([tall[heads : heads + 2], jnp.zeros((6, BLOCK), f32)], axis=0))
            own = dot(low_b, jnp.broadcast_to(two[:, 0:1], (BLOCK, BLOCK)))
            other = dot(jnp.broadcast_to(mark, (BLOCK, BLOCK)), up_b)
            mask_ref[n] = jnp.where(own == other, low, 0.0)
            alive_ref[n] = (own == 0).astype(f32)
            lasts[n] = (own == other[:, BLOCK - 1 : BLOCK]).astype(f32)
            kinds[n] = jnp.broadcast_to(two[:, 1:2], (BLOCK, BLOCK))
            gates[n] = jnp.concatenate(
                [chunk(s, j) for s in range(n * per, (n + 1) * per) for j in range(tok // 16)], axis=0
            )

    low2 = jnp.concatenate([low_b, low_b], axis=1)
    lower = (row > col).astype(f32)
    items = [(i, n) for i in range(hp) for n in range(blocks)]
    strict_all, rhs_all, tail_all, carry_all = {}, {}, {}, {}
    betas = []
    for n in range(blocks):
        mine = values[n, pl.ds(start, hp), :]
        betas.append(jnp.transpose(jnp.concatenate([mine, jnp.zeros((8 - hp % 8, BLOCK), f32)], axis=0)))
    for i in range(hp):
        h = start + i
        at = pl.ds(pl.multiple_of(h * DK, DK), DK)
        bias_at = pl.ds(pl.multiple_of(me * width + h * DK, DK), DK)
        audio, text = bias_ref[0:1, bias_at], bias_ref[1:2, bias_at]
        rate = -LOG2E * jnp.exp(jnp.full((1, DK), decay_ref[me * heads + h], f32))
        for n in range(blocks):
            gate = dot(gates[n], up[:, at]).astype(bf16).astype(f32)
            pre = gate + jnp.where(kinds[n] == 1.0, text, audio)
            soft = jnp.maximum(pre, 0.0) + jnp.log(1.0 + jnp.exp(-jnp.abs(pre)))
            high, rest_part = split(rate * soft)
            total = dot(low2, jnp.concatenate([high, rest_part], axis=0))
            key = buf[n * per : (n + 1) * per, 0:tok, at].reshape(BLOCK, DK).astype(f32)
            value = buf[n * per : (n + 1) * per, tok : 2 * tok, at].reshape(BLOCK, DK).astype(f32)
            unit = key * lax.rsqrt(jnp.sum(key * key, axis=1, keepdims=True) + norm_eps)
            growth = jnp.exp2(total)
            grown = unit * growth
            shrunk, shrunk_rest = split(unit * jnp.exp2(-total))
            last = total[BLOCK - 1 : BLOCK]
            tail = unit * (jnp.exp2(last - total) * lasts[n])
            carry = jnp.exp2(last) * alive_ref[n, BLOCK - 1 : BLOCK]
            beta = jnp.broadcast_to(betas[n][:, i : i + 1], (BLOCK, BLOCK))
            growth_ref[i, n] = growth
            shrink_ref[i, n, :, :DK] = shrunk
            shrink_ref[i, n, :, DK:] = shrunk_rest
            gram = dot(grown, shrunk, NT)
            strict_all[i, n] = (gram * (mask_ref[n] * lower) * beta).astype(bf16)
            rhs_all[i, n] = jnp.concatenate([beta * grown * alive_ref[n], beta * value], axis=1)
            tail_all[i, n] = jnp.transpose(tail)
            carry_all[i, n] = carry
    turned = jnp.transpose(jnp.concatenate([carry_all[t] for t in items] + [jnp.zeros((BLOCK - len(items), DK), f32)]))
    carry_all = {t: turned[:, j : j + 1] for j, t in enumerate(items)}
    inv = {t: unit_mat - strict_all[t] * levels[0] for t in items}
    for level in range(1, count):
        size = 2**level
        corner = {t: strict_all[t] * levels[level] for t in items}
        if size < 16:
            turn = {t: dot(inv[t], corner[t]) for t in items}
            inv = {t: inv[t] - dot(turn[t], inv[t]).astype(bf16) for t in items}
        else:
            pairs = BLOCK // (2 * size)
            four = {t: inv[t].reshape(pairs, 2, size, BLOCK) for t in items}
            odd = {t: four[t][:, 1].reshape(BLOCK // 2, BLOCK) for t in items}
            turn = {t: dot(odd[t], corner[t]) for t in items}
            odd = {t: odd[t] - dot(turn[t], inv[t]).astype(bf16) for t in items}
            inv = {
                t: jnp.stack([four[t][:, 0], odd[t].reshape(pairs, size, BLOCK)], axis=1).reshape(BLOCK, BLOCK)
                for t in items
            }
    both = {t: rhs_all[t] + dot(inv[t] - unit_mat, rhs_all[t]) for t in items}
    fade, offs = {}, {}
    for t in items:
        i, n = t
        w = both[t][:, :DK].astype(bf16)
        w_ref[i, n] = w
        u_ref[i, n] = both[t][:, DK:]
        uh, ul = split(both[t][:, DK:])
        th, tl = split(tail_all[t])
        joint = dot(th, jnp.concatenate([w, uh], axis=1))
        fade[t] = joint[:, :DK]
        offs[t] = joint[:, DK:] + dot(jnp.concatenate([th, tl], axis=1), jnp.concatenate([ul, uh], axis=0))
    offset = {i: offs[i, 0] for i in range(hp)}
    move = {i: jnp.where(row == col, carry_all[i, 0], 0.0) - fade[i, 0] for i in range(hp)}
    for n in range(1, blocks):
        for i in range(hp):
            opre_ref[i, n - 1] = offset[i]
            mpre_ref[i, n - 1] = move[i].astype(bf16)
            joint = dot(fade[i, n], jnp.concatenate([offset[i], move[i]], axis=1))
            offset[i] = carry_all[i, n] * offset[i] + offs[i, n] - joint[:, :DK]
            move[i] = carry_all[i, n] * move[i] - joint[:, DK:]
    for i in range(hp):
        span_ref[i] = jnp.concatenate([offset[i], move[i]], axis=1).astype(bf16)


def joined(later, earlier):
    both = dot(later[1], jnp.concatenate([earlier[0], earlier[1]], axis=1))
    return (later[0].astype(f32) + both[:, :DK]).astype(bf16), both[:, DK:].astype(bf16)


def ordered(outer, parts, order):
    hi = lax.div(lax.axis_index("head"), lax.axis_size("head") // outer)
    for j in range(outer):
        order[hi ^ j] = parts[j][...]


def compose_kernel(outer, share, *rest):
    parts, out_ref, order = rest[:outer], rest[-2], rest[-1]
    ordered(outer, parts, order)
    for h in range(share):
        whole = (order[0, h, :, :DK], order[0, h, :, DK:])
        for o in range(1, outer):
            whole = joined((order[o, h, :, :DK], order[o, h, :, DK:]), whole)
        out_ref[h, :, :DK] = whole[0]
        out_ref[h, :, DK:] = whole[1]


def relay_kernel(share, whole_ref, got_ref, out_ref):
    for h in range(share):
        whole = joined(
            (whole_ref[h, :, :DK], whole_ref[h, :, DK:]), (got_ref[h, :, :DK], got_ref[h, :, DK:])
        )
        out_ref[h, :, :DK] = whole[0]
        if out_ref.shape[2] > DK:
            out_ref[h, :, DK:] = whole[1]


def seed_kernel(outer, share, raw, *rest):
    parts = rest[:outer]
    early_ref, in_ref = rest[outer : outer + 2]
    outs = rest[outer + 2 : 2 * outer + 2]
    order, seeds = rest[2 * outer + 2 :]
    hi = lax.div(lax.axis_index("head"), lax.axis_size("head") // outer)
    ordered(outer, parts, order)
    row = lax.broadcasted_iota(jnp.int32, (DK, DK), 0)
    col = lax.broadcasted_iota(jnp.int32, (DK, DK), 1)
    odd = lax.rem(lax.axis_index("seq"), 2) == 1
    for h in range(share):
        incoming = in_ref[h]
        through = dot(early_ref[h, :, DK:], incoming)
        if raw:
            through = jnp.where(odd, through, incoming.astype(f32))
        state = (early_ref[h, :, :DK].astype(f32) + through).astype(bf16)
        seeds[0, h] = state
        for o in range(1, outer):
            moved = dot(order[o - 1, h, :, DK:], state)
            state = (order[o - 1, h, :, :DK].astype(f32) + moved).astype(bf16)
            seeds[o, h] = state
    for j in range(outer):
        outs[j][...] = seeds[hi ^ j]


def query_kernel(sub, outer, first, blocks, heads, tok, batch, hp, *rest):
    pieces = rest[:sub]
    w_ref, u_ref, shrink_ref, growth_ref, mask_ref, alive_ref = rest[sub : sub + 6]
    base_ref, rows_ref, buf, sem = rest[-4:]
    lo = lax.rem(lax.axis_index("head"), sub)
    per = BLOCK // tok

    @pl.when(pl.program_id(0) == 0)
    def _():
        copies = [
            pltpu.make_async_copy(pieces[k].at[pl.ds(batch * tok, tok)], buf.at[lo ^ k], sem.at[k])
            for k in range(sub)
        ]
        for c in copies:
            c.start()
        for c in copies:
            c.wait()

    items = [(i, n) for i in range(hp) for n in range(blocks)]
    start = place(outer, first, heads // outer, hp)
    at = [pl.ds(pl.multiple_of((start + i) * DK, DK), DK) for i in range(hp)]
    grown, mix = {}, {}
    for i, n in items:
        query = buf[n * per : (n + 1) * per, :, at[i]].reshape(BLOCK, DK).astype(f32)
        unit = query * (lax.rsqrt(jnp.sum(query * query, axis=1, keepdims=True) + norm_eps) * DK ** (-0.5))
        grown[i, n] = unit * growth_ref[i, n]
        gh, gl = split(grown[i, n])
        shrunk = shrink_ref[i, n]
        mix[i, n] = mask_ref[n] * dot(
            jnp.concatenate([gh, gh, gl], axis=1), jnp.concatenate([shrunk, shrunk[:, :DK]], axis=1), NT
        )
    for i, n in items:
        mh, ml = split(mix[i, n])
        uh, ul = split(u_ref[i, n])
        both = dot(mh, jnp.concatenate([uh, w_ref[i, n]], axis=1))
        rest_part = dot(jnp.concatenate([mh, ml], axis=1), jnp.concatenate([ul, uh], axis=0))
        base_ref[i, n] = both[:, :DK] + rest_part
        rows_ref[i, n] = (grown[i, n] * alive_ref[n] - both[:, DK:]).astype(bf16)


def output_kernel(sub, outer, sets, blocks, heads, tok, *rest):
    seeds, rest = rest[:outer], rest[outer:]
    outs, obuf = rest[-sub - 1 : -1], rest[-1]
    lo = lax.rem(lax.axis_index("head"), sub)
    hi = lax.div(lax.axis_index("head"), sub)
    share = heads // outer
    per = BLOCK // tok
    for part, (first, shares) in enumerate(sets):
        base_ref, rows_ref, opre_ref, mpre_ref = rest[4 * part : 4 * part + 4]
        for r in range(shares * share):
            j, i = first + r // share, r % share
            at = pl.ds(pl.multiple_of(((hi ^ j) * share + i) * DK, DK), DK)
            seed = seeds[j][i]
            for n in range(blocks):
                state = seed if n == 0 else opre_ref[r, n - 1] + dot(mpre_ref[r, n - 1], seed)
                core = base_ref[r, n] + dot(rows_ref[r, n], state)
                obuf[n * per : (n + 1) * per, :, at] = core.astype(bf16).reshape(per, tok, DK)
    for k in range(sub):
        outs[k][...] = obuf[lo ^ k]


def finish_kernel(sub, heads, *rest):
    pieces = rest[:sub]
    gate_ref, gain_ref = rest[sub : sub + 2]
    out_ref = rest[-1]
    me = lax.rem(lax.axis_index("head"), sub)
    for k in range(sub):
        for h in range(heads):
            at = pl.ds(pl.multiple_of((me ^ k) * (heads * DK) + h * DK, DK), DK)
            core = pieces[k][:, h * DK : (h + 1) * DK].astype(f32)
            normed = core * lax.rsqrt(jnp.mean(core * core, axis=1, keepdims=True) + norm_eps)
            out_ref[0, :, at] = (normed * gain_ref[:, at] * jax.nn.sigmoid(gate_ref[0, :, at].astype(f32))).astype(bf16)


def product(a, b):
    return jnp.einsum("hij,hjk->hik", a, b, preferred_element_type=f32)


def before(span):
    count = lax.axis_size("seq")
    place = lax.axis_index("seq")
    unit_mat = jnp.broadcast_to(jnp.eye(DK, dtype=bf16), span.shape[:1] + (DK, DK))
    raw = True
    early, whole = None, span
    size = 1
    while size < count:
        final = 2 * size >= count
        payload = whole[..., :DK] if final and size == 1 else whole
        got = None
        for t in range(size):
            pairs = [
                (base + size - 1, base + size + t)
                for base in range(0, count, 2 * size)
                if base + size + t < count
            ]
            part = lax.ppermute(payload, "seq", pairs)
            got = part if got is None else got + part
        if final:
            break
        right = (place // size) % 2 == 1
        if size == 1:
            early = got
        else:
            e_move = early[..., DK:]
            if raw:
                e_move = jnp.where(place % 2 == 1, e_move, unit_mat)
            raw = False
            moved = product(e_move, got)
            early = jnp.concatenate(
                [
                    (early[..., :DK].astype(f32) + moved[..., :DK]).astype(bf16),
                    jnp.where(right, moved[..., DK:].astype(bf16), e_move),
                ],
                axis=2,
            )
        share = whole.shape[0]
        last = 4 * size >= count
        whole = pl.pallas_call(
            functools.partial(relay_kernel, share),
            out_shape=jax.ShapeDtypeStruct((share, DK, DK if last else 2 * DK), bf16),
            in_specs=[VMEM] * 2,
            out_specs=VMEM,
            compiler_params=params(),
            cost_estimate=cost(0, 0),
            name=f"relay_{size}",
        )(whole, got)
        size *= 2
    if early is None:
        early = jnp.concatenate([jnp.zeros_like(unit_mat), unit_mat], axis=2)
    return early, got, raw


def per_device(
    query_rows,
    key_rows,
    value_rows,
    beta_raw,
    gate_latent,
    gate_up,
    dt_bias,
    decay_log,
    boundary,
    modality,
    out_gate,
    norm_gain,
):
    places = lax.axis_size("head")
    batches, tok, columns = query_rows.shape
    sub = min(places, 4)
    outer = places // sub
    total_heads = columns // DK
    heads = total_heads // sub
    share = heads // outer
    width = heads * DK
    blocks = tok * sub // BLOCK
    sds = jax.ShapeDtypeStruct
    extra_rows = 16 * -(-(tok // 16 + misc_rows(heads) // 16) // (width // 128))
    piece_rows = 2 * tok + extra_rows

    def pack_kv(batch, *after):
        return pl.pallas_call(
            functools.partial(pack_kv_kernel, sub, batch, heads),
            out_shape=[sds((piece_rows, width), bf16)] * sub,
            in_specs=[ANY] * (6 + len(after)),
            out_specs=[VMEM] * sub,
            scratch_shapes=[
                pltpu.VMEM(gate_latent.shape[1:], bf16),
                pltpu.VMEM(beta_raw.shape[1:], bf16),
                pltpu.VMEM(boundary.shape, jnp.int32),
                pltpu.VMEM(modality.shape, jnp.int32),
                pltpu.VMEM((128, 128), f32),
                pltpu.SemaphoreType.DMA((sub, 3)),
                pltpu.SemaphoreType.DMA((4,)),
            ],
            compiler_params=params(PACK_MIB),
            cost_estimate=cost(0, 0),
            name=f"pack_kv_{batch}",
        )(key_rows, value_rows, gate_latent, beta_raw, boundary, modality, *after)

    kv = []
    for b in range(batches):
        kv.append(exchange(pack_kv(b, *([] if b == 0 else [kv[-1][-1]]))))
    hp = min(share, max(1, 8 // blocks))
    while share % hp:
        hp -= 1
    before_rows = max(1, blocks - 1)

    def by_head(*dims):
        return pl.BlockSpec((hp, *dims), lambda i: (i,) + (0,) * len(dims))

    per_head = by_head(blocks, DK, DK)
    wide_head = by_head(blocks, DK, 2 * DK)
    pre_head = by_head(before_rows, DK, DK)
    whole = pl.BlockSpec((blocks, BLOCK, BLOCK), lambda i: (0, 0, 0))
    levels = BLOCK.bit_length() - 1
    local_dims = [
        ((blocks, DK, DK), bf16),
        ((blocks, DK, DK), f32),
        ((blocks, DK, 2 * DK), bf16),
        ((blocks, DK, DK), f32),
        ((before_rows, DK, DK), f32),
        ((before_rows, DK, DK), bf16),
        ((DK, 2 * DK), bf16),
    ]
    count = lax.axis_size("head")

    def state_maps(b, first, shares, *after):
        here = shares * share
        return pl.pallas_call(
            functools.partial(state_kernel, sub, outer, first, blocks, heads, tok, hp),
            grid=(here // hp,),
            out_shape=[sds((here, *dims), kind) for dims, kind in local_dims] + [sds((blocks, BLOCK, BLOCK), f32)] * 2,
            in_specs=[SMEM] + [ANY] * sub + [ANY, VMEM] + [ANY] * len(after),
            out_specs=[by_head(*dims) for dims, _ in local_dims] + [whole, whole],
            scratch_shapes=[
                pltpu.VMEM((sub, piece_rows, width), bf16),
                pltpu.VMEM((DK, width), bf16),
                pltpu.VMEM((levels, BLOCK, BLOCK), bf16),
                pltpu.VMEM((blocks, BLOCK, BLOCK), f32),
                pltpu.VMEM((blocks, BLOCK, BLOCK), f32),
                pltpu.VMEM((blocks, misc_rows(heads), BLOCK), f32),
                pltpu.VMEM((blocks, BLOCK, BLOCK), bf16),
                pltpu.SemaphoreType.DMA((sub + 1,)),
            ],
            compiler_params=params(),
            cost_estimate=cost(SCALE * here * blocks * 2e8, 0),
            name=f"state_maps_{b}_{first}",
        )(decay_log, *kv[b], gate_up, dt_bias, *after)

    def swap(parts):
        return [parts[0]] + [
            lax.ppermute(parts[j], "head", [(i, i ^ (j * sub)) for i in range(count)]) for j in range(1, outer)
        ]

    sets = ([(1, outer - 1)] if outer > 1 else []) + [(0, 1)]
    local, split_maps = [], []
    q_here = None
    for b in range(batches):
        made = []
        for first, shares in sets:
            after = [kv[b + 1][0]] if first == sets[0][0] and b + 1 < batches else []
            made.append(state_maps(b, first, shares, *after))
        local.append(made)
        sent = []
        if outer > 1:
            spans = made[0][6]
            sent = [spans] if outer == 2 else [spans[j * share : (j + 1) * share] for j in range(outer - 1)]
        split_maps.append(swap([made[-1][6]] + sent))
        if q_here is None:
            q_here = exchange(
                pl.pallas_call(
                    functools.partial(pack_q_kernel, sub, batches),
                    out_shape=[sds((batches * tok, width), bf16)] * sub,
                    in_specs=[ANY, ANY],
                    out_specs=[VMEM] * sub,
                    scratch_shapes=[pltpu.SemaphoreType.DMA((sub, batches))],
                    compiler_params=params(),
                    cost_estimate=cost(0, 0),
                    name="pack_q",
                )(query_rows, kv[-1][-1])
            )
    queries = []
    for b in range(batches):
        made = []
        for (first, shares), here in zip(sets, local[b]):
            made.append(
                pl.pallas_call(
                    functools.partial(query_kernel, sub, outer, first, blocks, heads, tok, b, hp),
                    grid=(shares * share // hp,),
                    out_shape=[
                        sds((shares * share, blocks, DK, DK), f32),
                        sds((shares * share, blocks, DK, DK), bf16),
                    ],
                    in_specs=[ANY] * sub + [per_head, per_head, wide_head, per_head] + [whole] * 2,
                    out_specs=[per_head] * 2,
                    scratch_shapes=[pltpu.VMEM((sub, tok, width), bf16), pltpu.SemaphoreType.DMA((sub,))],
                    compiler_params=params(),
                    cost_estimate=cost(SCALE * shares * share * blocks * 1e8, 0),
                    name=f"query_parts_{b}_{first}",
                )(*q_here, *here[:4], *here[7:9])
            )
        queries.append(made)
    back = []
    for b in range(batches):
        parts = split_maps[b]
        after = [made[1] for made in queries[-1]] if b == batches - 1 else []
        total = pl.pallas_call(
            functools.partial(compose_kernel, outer, share),
            out_shape=sds((share, DK, 2 * DK), bf16),
            in_specs=[VMEM] * outer + [ANY] * len(after),
            out_specs=VMEM,
            scratch_shapes=[pltpu.VMEM((outer, share, DK, 2 * DK), bf16)],
            compiler_params=params(),
            cost_estimate=cost(0, 0),
            name=f"compose_{b}",
        )(*parts, *after)
        early, incoming, raw = before(total)
        mine = pl.pallas_call(
            functools.partial(seed_kernel, outer, share, raw),
            out_shape=[sds((share, DK, DK), bf16)] * outer,
            in_specs=[VMEM] * (outer + 2),
            out_specs=[VMEM] * outer,
            scratch_shapes=[
                pltpu.VMEM((outer, share, DK, 2 * DK), bf16),
                pltpu.VMEM((outer, share, DK, DK), bf16),
            ],
            compiler_params=params(),
            cost_estimate=cost(0, 0),
            name=f"seeds_{b}",
        )(*parts, early, incoming)
        operands = []
        for made, here in zip(queries[b], local[b]):
            operands += [*made, *here[4:6]]
        outs = pl.pallas_call(
            functools.partial(output_kernel, sub, outer, sets, blocks, heads, tok),
            out_shape=[sds((tok, width), bf16)] * sub,
            in_specs=[VMEM] * (len(operands) + outer),
            out_specs=[VMEM] * sub,
            scratch_shapes=[pltpu.VMEM((sub, tok, width), bf16)],
            compiler_params=params(),
            cost_estimate=cost(SCALE * heads * blocks * 2e7, 0),
            name=f"span_outputs_{b}",
        )(*swap(mine), *operands)
        back.append(exchange(outs))

    mixed = None
    for b in range(batches):
        rows = pl.BlockSpec((1, tok, columns), lambda i, b=b: (b, 0, 0))
        mixed = pl.pallas_call(
            functools.partial(finish_kernel, sub, heads),
            grid=(1,),
            out_shape=sds((batches, tok, columns), bf16),
            in_specs=[pl.BlockSpec((tok, width), lambda i: (0, 0))] * sub
            + [rows, pl.BlockSpec((1, columns), lambda i: (0, 0))]
            + ([] if b == 0 else [ANY]),
            out_specs=rows,
            input_output_aliases={} if b == 0 else {sub + 2: 0},
            compiler_params=params(),
            cost_estimate=cost(0, 0),
            name=f"finish_{b}",
        )(*back[b], out_gate, norm_gain[None, :], *([] if b == 0 else [mixed]))
    return mixed


def solution(mesh):
    return jax.shard_map(
        per_device,
        mesh=mesh,
        in_specs=(
            P(None, ("seq", "head"), None),
            P(None, ("seq", "head"), None),
            P(None, ("seq", "head"), None),
            P(None, ("seq", "head"), None),
            P(None, ("seq", "head"), None),
            P(),
            P(),
            P(),
            P(None, ("seq", "head")),
            P(None, ("seq", "head")),
            P(None, ("seq", "head"), None),
            P(),
        ),
        out_specs=P(None, ("seq", "head"), None),
        check_vma=False,
    )
```

```python
import functools

import jax
import jax.numpy as jnp
from jax import lax
from jax.experimental import pallas as pl
from jax.experimental.pallas import tpu as pltpu
from jax.sharding import PartitionSpec as P

DK = 128
BLOCK = 128
norm_eps = 1e-06
LOG2E = 1.4426950408889634
f32 = jnp.float32
bf16 = jnp.bfloat16
ANY = pl.BlockSpec(memory_space=pl.ANY)
VMEM = pl.BlockSpec(memory_space=pltpu.VMEM)
SMEM = pl.BlockSpec(memory_space=pltpu.SMEM)
SCALE = 0.1


def params(mib=48):
    return pltpu.CompilerParams(vmem_limit_bytes=mib * 1024 * 1024)


def misc_rows(heads):
    return -(-(heads + 2) // 16) * 16


def cost(flops, nbytes):
    return pl.CostEstimate(flops=int(flops), bytes_accessed=int(nbytes), transcendentals=0)


def dot(a, b, dims=((1,), (0,))):
    return lax.dot_general(
        a.astype(bf16), b.astype(bf16), (dims, ((), ())), preferred_element_type=f32
    )


def split(a):
    high = a.astype(bf16)
    return high, (a - high.astype(f32)).astype(bf16)


def dot3(a, b, dims=((1,), (0,))):
    ah, al = split(a)
    bh, bl = split(b)
    return dot(ah, bh, dims) + (dot(ah, bl, dims) + dot(al, bh, dims))


NT = ((1,), (1,))


def pack_kv_kernel(sub, outer, batches, heads, first, extras, key_ref, value_ref, latent_ref, beta_ref, mark_ref, kind_ref, *rest):
    outs, (latent, beta, mark, kind, wide, sem, small_sem) = rest[-sub - 7 : -7], rest[-7:]
    lo = lax.rem(lax.axis_index("head"), sub)
    hi = lax.div(lax.axis_index("head"), sub)
    rows, width = key_ref.shape[1], outs[0].shape[1]
    part = heads // outer * DK
    copies = []
    for k in range(sub):
        for j in range(width // part):
            col = pl.multiple_of(((lo ^ k) * outer + (hi ^ ((first + j) % outer))) * part, part)
            for n, batch in enumerate(batches):
                for i, ref in enumerate((key_ref, value_ref)):
                    copies.append(
                        pltpu.make_async_copy(
                            ref.at[batch, :, pl.ds(col, part)],
                            outs[k].at[pl.ds((2 * n + i) * rows, rows), pl.ds(j * part, part)],
                            sem.at[k, j, 2 * n + i],
                        )
                    )
                    copies[-1].start()
    if extras:
        (batch,) = batches
        small = [
            pltpu.make_async_copy(source, target, small_sem.at[i])
            for i, (source, target) in enumerate(
                ((latent_ref.at[batch], latent), (beta_ref.at[batch], beta), (mark_ref, mark), (kind_ref, kind))
            )
        ]
        for c in small:
            c.start()
        for c in small:
            c.wait()
        lanes = width // 128
        misc = misc_rows(heads)
        wide[...] = beta[...].astype(f32)
        tokens = jnp.concatenate([mark[batch : batch + 1].astype(f32), kind[batch : batch + 1].astype(f32)], axis=0)
        for k in range(sub):
            own = wide[pl.ds(pl.multiple_of((lo ^ k) * heads, heads), heads), :]
            values = jnp.concatenate([own, tokens, jnp.zeros((misc - heads - 2, rows), f32)], axis=0)
            values = jnp.concatenate([values, jnp.zeros((misc, 128 - rows), f32)], axis=1).astype(bf16)
            chunks = [latent[16 * j : 16 * j + 16] for j in range(rows // 16)]
            chunks += [values[16 * j : 16 * j + 16] for j in range(misc // 16)]
            chunks += [jnp.zeros((16, 128), bf16)] * (-len(chunks) % lanes)
            for c, chunk in enumerate(chunks):
                at = 2 * rows + 16 * (c // lanes)
                outs[k][at : at + 16, (c % lanes) * 128 : (c % lanes + 1) * 128] = chunk
    for c in copies:
        c.wait()


def pack_q_kernel(sub, batches, query_ref, *rest):
    outs, sem = rest[-sub - 1 : -1], rest[-1]
    lo = lax.rem(lax.axis_index("head"), sub)
    rows, width = query_ref.shape[1], query_ref.shape[2] // sub
    copies = []
    for k in range(sub):
        col = pl.multiple_of((lo ^ k) * width, width)
        for b in range(batches):
            copies.append(
                pltpu.make_async_copy(
                    query_ref.at[b, :, pl.ds(col, width)], outs[k].at[pl.ds(b * rows, rows)], sem.at[k, b]
                )
            )
            copies[-1].start()
    for c in copies:
        c.wait()


def exchange(pieces):
    count = lax.axis_size("head")
    got = {
        k: lax.ppermute(pieces[k], "head", [(i, i ^ k) for i in range(count)]) for k in range(len(pieces) - 1, 0, -1)
    }
    return [pieces[0]] + [got[k] for k in range(1, len(pieces))]


def place(outer, first, share, hp):
    at = pl.program_id(0) * hp
    hi = lax.div(lax.axis_index("head"), lax.axis_size("head") // outer)
    return (hi ^ (first + lax.div(at, share))) * share + lax.rem(at, share)


def reorder(parts, place, bits):
    for bit in range(bits):
        flipped = lax.rem(lax.div(place, 2**bit), 2) == 1
        parts = [jnp.where(flipped, parts[i ^ 2**bit], parts[i]) for i in range(len(parts))]
    return parts


def token_rows(pieces, slot, lo, tok, load):
    per = BLOCK // tok
    parts = [load(pieces[slot * per + r]) for r in range(per)]
    return jnp.concatenate(reorder(parts, lax.rem(lo, per), per.bit_length() - 1), axis=0)


def state_kernel(sub, outer, first, lane, blocks, heads, tok, hp, decay_ref, *rest):
    pieces, extras = rest[:sub], rest[sub : 2 * sub]
    up_ref, bias_ref = rest[2 * sub : 2 * sub + 2]
    w_ref, u_ref, shrink_ref, growth_ref, opre_ref, mpre_ref, span_ref, mask_ref, alive_ref = rest[-14:-5]
    levels, kinds, lasts, values, gates = rest[-5:]
    me = lax.rem(lax.axis_index("head"), sub)
    start = place(outer, first, heads // outer, hp)
    width = heads * DK
    per = BLOCK // tok
    row = lax.broadcasted_iota(jnp.int32, (BLOCK, BLOCK), 0)
    col = lax.broadcasted_iota(jnp.int32, (BLOCK, BLOCK), 1)
    low = (row >= col).astype(f32)
    low_b = low.astype(bf16)
    up_b = (row <= col).astype(bf16)
    unit_mat = (row == col).astype(bf16)
    count = BLOCK.bit_length() - 1
    step = pl.program_id(0)

    @pl.when(step == 0)
    def _():
        for level in range(count):
            size = 2**level
            here = (row // size == col // size + 1) & ((row // size) % 2 == 1)
            levels[level] = here.astype(bf16)
        lanes = extras[0].shape[1] // 128
        misc = misc_rows(heads)

        def chunk(piece, c):
            at = 2 * tok + 16 * (c // lanes)
            return piece[at : at + 16, (c % lanes) * 128 : (c % lanes + 1) * 128]

        for n in range(blocks):
            parts = [
                jnp.concatenate(
                    [chunk(extras[n * per + r], tok // 16 + j).astype(f32) for j in range(misc // 16)], axis=0
                )[:, :tok]
                for r in range(per)
            ]
            tall = jnp.concatenate(reorder(parts, lax.rem(me, per), per.bit_length() - 1), axis=1)
            values[n] = jax.nn.sigmoid(tall)
            mark = tall[heads : heads + 1]
            two = jnp.transpose(jnp.concatenate([tall[heads : heads + 2], jnp.zeros((6, BLOCK), f32)], axis=0))
            own = dot(low_b, jnp.broadcast_to(two[:, 0:1], (BLOCK, BLOCK)))
            other = dot(jnp.broadcast_to(mark, (BLOCK, BLOCK)), up_b)
            mask_ref[n] = jnp.where(own == other, low, 0.0)
            alive_ref[n] = (own == 0).astype(f32)
            lasts[n] = (own == other[:, BLOCK - 1 : BLOCK]).astype(f32)
            kinds[n] = jnp.broadcast_to(two[:, 1:2], (BLOCK, BLOCK))
            gates[n] = token_rows(
                extras, n, me, tok, lambda p: jnp.concatenate([chunk(p, j) for j in range(tok // 16)], axis=0)
            )

    low2 = jnp.concatenate([low_b, low_b], axis=1)
    lower = (row > col).astype(f32)
    items = [(i, n) for i in range(hp) for n in range(blocks)]
    every = range(blocks)
    strict_all, rhs_all, tail_all, carry_all = {}, {}, {}, {}
    betas = []
    for n in range(blocks):
        mine = values[n, pl.ds(start, hp), :]
        betas.append(jnp.transpose(jnp.concatenate([mine, jnp.zeros((8 - hp % 8, BLOCK), f32)], axis=0)))
    for i in range(hp):
        h = start + i
        at = pl.ds(pl.multiple_of(lane + (step * hp + i) * DK, DK), DK)
        bias_at = pl.ds(pl.multiple_of(me * width + h * DK, DK), DK)
        audio, text = bias_ref[0:1, bias_at], bias_ref[1:2, bias_at]
        rate = -LOG2E * jnp.exp(jnp.full((1, DK), decay_ref[me * heads + h], f32))
        for n in range(blocks):
            gate = dot(gates[n], up_ref[:, bias_at]).astype(bf16).astype(f32)
            pre = gate + jnp.where(kinds[n] == 1.0, text, audio)
            soft = jnp.maximum(pre, 0.0) + jnp.log(1.0 + jnp.exp(-jnp.abs(pre)))
            high, rest_part = split(rate * soft)
            total = dot(low2, jnp.concatenate([high, rest_part], axis=0))
            key = token_rows(pieces, n, me, tok, lambda p: p[0:tok, at]).astype(f32)
            value = token_rows(pieces, n, me, tok, lambda p: p[tok : 2 * tok, at]).astype(f32)
            unit = key * lax.rsqrt(jnp.sum(key * key, axis=1, keepdims=True) + norm_eps)
            growth = jnp.exp2(total)
            grown = unit * growth
            shrunk, shrunk_rest = split(unit * jnp.exp2(-total))
            last = total[BLOCK - 1 : BLOCK]
            tail = unit * (jnp.exp2(last - total) * lasts[n])
            carry = jnp.exp2(last) * alive_ref[n, BLOCK - 1 : BLOCK]
            beta = jnp.broadcast_to(betas[n][:, i : i + 1], (BLOCK, BLOCK))
            growth_ref[i, n] = growth
            shrink_ref[i, n, :, :DK] = shrunk
            shrink_ref[i, n, :, DK:] = shrunk_rest
            gram = dot(grown, shrunk, NT)
            strict_all[i, n] = (gram * (mask_ref[n] * lower) * beta).astype(bf16)
            rhs_all[i, n] = jnp.concatenate([beta * grown * alive_ref[n], beta * value], axis=1)
            tail_all[i, n] = jnp.transpose(tail)
            carry_all[i, n] = carry
    turned = jnp.transpose(jnp.concatenate([carry_all[t] for t in items] + [jnp.zeros((BLOCK - len(items), DK), f32)]))
    carry_all = {t: turned[:, j : j + 1] for j, t in enumerate(items)}
    inv = {t: unit_mat - strict_all[t] * levels[0] for t in items}
    for level in range(1, count):
        size = 2**level
        corner = {t: strict_all[t] * levels[level] for t in items}
        if size < 16:
            turn = {t: dot(inv[t], corner[t]) for t in items}
            inv = {t: inv[t] - dot(turn[t], inv[t]).astype(bf16) for t in items}
        else:
            pairs = BLOCK // (2 * size)
            four = {t: inv[t].reshape(pairs, 2, size, BLOCK) for t in items}
            odd = {t: four[t][:, 1].reshape(BLOCK // 2, BLOCK) for t in items}
            turn = {t: dot(odd[t], corner[t]) for t in items}
            odd = {t: odd[t] - dot(turn[t], inv[t]).astype(bf16) for t in items}
            inv = {
                t: jnp.stack([four[t][:, 0], odd[t].reshape(pairs, size, BLOCK)], axis=1).reshape(BLOCK, BLOCK)
                for t in items
            }
    both = {t: rhs_all[t] + dot(inv[t] - unit_mat, rhs_all[t]) for t in items}
    fade, offs = {}, {}
    for t in items:
        i, n = t
        w = both[t][:, :DK].astype(bf16)
        w_ref[i, n] = w
        u_ref[i, n] = both[t][:, DK:]
        uh, ul = split(both[t][:, DK:])
        th, tl = split(tail_all[t])
        joint = dot(th, jnp.concatenate([w, uh], axis=1))
        fade[t] = joint[:, :DK].astype(bf16)
        offs[t] = joint[:, DK:] + dot(jnp.concatenate([th, tl], axis=1), jnp.concatenate([ul, uh], axis=0))
    bits = blocks.bit_length() - 1
    for i in range(hp):
        for made in (fade, offs, carry_all):
            in_time = reorder([made[i, n] for n in every], lax.div(me, per), bits)
            for n in every:
                made[i, n] = in_time[n]
    offset = {i: offs[i, 0] for i in range(hp)}
    move = {i: jnp.where(row == col, carry_all[i, 0], 0.0) - fade[i, 0].astype(f32) for i in range(hp)}
    for n in range(1, blocks):
        for i in range(hp):
            opre_ref[i, n - 1] = offset[i]
            mpre_ref[i, n - 1] = move[i].astype(bf16)
            joint = dot(fade[i, n], jnp.concatenate([offset[i], move[i]], axis=1))
            offset[i] = carry_all[i, n] * offset[i] + offs[i, n] - joint[:, :DK]
            move[i] = carry_all[i, n] * move[i] - joint[:, DK:]
    for i in range(hp):
        span_ref[i] = jnp.concatenate([offset[i], move[i]], axis=1).astype(bf16)


def joined(later, earlier):
    both = dot(later[1], jnp.concatenate([earlier[0], earlier[1]], axis=1))
    return (later[0].astype(f32) + both[:, :DK]).astype(bf16), both[:, DK:].astype(bf16)


def ordered(outer, parts, order):
    hi = lax.div(lax.axis_index("head"), lax.axis_size("head") // outer)
    for j in range(outer):
        order[hi ^ j] = parts[j][...]


def compose_kernel(outer, share, *rest):
    parts, out_ref, order = rest[:outer], rest[-2], rest[-1]
    ordered(outer, parts, order)
    for h in range(share):
        whole = (order[0, h, :, :DK], order[0, h, :, DK:])
        for o in range(1, outer):
            whole = joined((order[o, h, :, :DK], order[o, h, :, DK:]), whole)
        out_ref[h, :, :DK] = whole[0]
        out_ref[h, :, DK:] = whole[1]


def relay_kernel(share, whole_ref, got_ref, *rest):
    out_ref = rest[-1]
    for h in range(share):
        whole = joined(
            (whole_ref[h, :, :DK], whole_ref[h, :, DK:]), (got_ref[h, :, :DK], got_ref[h, :, DK:])
        )
        out_ref[h, :, :DK] = whole[0]
        if out_ref.shape[2] > DK:
            out_ref[h, :, DK:] = whole[1]


def seed_kernel(outer, share, raw, *rest):
    parts = rest[:outer]
    early_ref, in_ref = rest[outer : outer + 2]
    outs, (order, seeds) = rest[-outer - 2 : -2], rest[-2:]
    hi = lax.div(lax.axis_index("head"), lax.axis_size("head") // outer)
    ordered(outer, parts, order)
    row = lax.broadcasted_iota(jnp.int32, (DK, DK), 0)
    col = lax.broadcasted_iota(jnp.int32, (DK, DK), 1)
    odd = lax.rem(lax.axis_index("seq"), 2) == 1
    for h in range(share):
        incoming = in_ref[h]
        through = dot(early_ref[h, :, DK:], incoming)
        if raw:
            through = jnp.where(odd, through, incoming.astype(f32))
        state = (early_ref[h, :, :DK].astype(f32) + through).astype(bf16)
        seeds[0, h] = state
        for o in range(1, outer):
            moved = dot(order[o - 1, h, :, DK:], state)
            state = (order[o - 1, h, :, :DK].astype(f32) + moved).astype(bf16)
            seeds[o, h] = state
    for j in range(outer):
        outs[j][...] = seeds[hi ^ j]


def query_kernel(sub, outer, first, blocks, heads, tok, batch, hp, *rest):
    pieces = rest[:sub]
    w_ref, u_ref, shrink_ref, growth_ref, mask_ref, alive_ref = rest[sub : sub + 6]
    base_ref, rows_ref = rest[-2:]
    lo = lax.rem(lax.axis_index("head"), sub)
    items = [(i, n) for i in range(hp) for n in range(blocks)]
    start = place(outer, first, heads // outer, hp)
    at = [pl.ds(pl.multiple_of((start + i) * DK, DK), DK) for i in range(hp)]
    grown, mix = {}, {}
    for i, n in items:
        query = token_rows(pieces, n, lo, tok, lambda p: p[batch * tok : (batch + 1) * tok, at[i]]).astype(f32)
        unit = query * (lax.rsqrt(jnp.sum(query * query, axis=1, keepdims=True) + norm_eps) * DK ** (-0.5))
        grown[i, n] = unit * growth_ref[i, n]
        gh, gl = split(grown[i, n])
        shrunk = shrink_ref[i, n]
        mix[i, n] = mask_ref[n] * dot(
            jnp.concatenate([gh, gh, gl], axis=1), jnp.concatenate([shrunk, shrunk[:, :DK]], axis=1), NT
        )
    for i, n in items:
        mh, ml = split(mix[i, n])
        uh, ul = split(u_ref[i, n])
        both = dot(mh, jnp.concatenate([uh, w_ref[i, n]], axis=1))
        rest_part = dot(jnp.concatenate([mh, ml], axis=1), jnp.concatenate([ul, uh], axis=0))
        base_ref[i, n] = both[:, :DK] + rest_part
        rows_ref[i, n] = (grown[i, n] * alive_ref[n] - both[:, DK:]).astype(bf16)


def output_kernel(sub, outer, sets, blocks, heads, tok, *rest):
    seeds, rest = rest[:outer], rest[outer:]
    outs = rest[-sub:]
    lo = lax.rem(lax.axis_index("head"), sub)
    hi = lax.div(lax.axis_index("head"), sub)
    share = heads // outer
    per = BLOCK // tok
    for part, (first, shares) in enumerate(sets):
        base_ref, rows_ref, opre_ref, mpre_ref = rest[4 * part : 4 * part + 4]
        for r in range(shares * share):
            j, i = first + r // share, r % share
            at = pl.ds(pl.multiple_of(((hi ^ j) * share + i) * DK, DK), DK)
            seed = seeds[j][i]
            states = [seed] + [
                (opre_ref[r, n] + dot(mpre_ref[r, n], seed)).astype(bf16) for n in range(blocks - 1)
            ]
            states = reorder(states, lax.div(lo, per), blocks.bit_length() - 1)
            for n in range(blocks):
                core = (base_ref[r, n] + dot(rows_ref[r, n], states[n])).astype(bf16)
                rows = reorder([core[t * tok : (t + 1) * tok] for t in range(per)], lax.rem(lo, per), per.bit_length() - 1)
                for t in range(per):
                    outs[n * per + t][:, at] = rows[t]


def finish_kernel(sub, heads, *rest):
    pieces = rest[:sub]
    gate_ref, gain_ref = rest[sub : sub + 2]
    out_ref = rest[-1]
    me = lax.rem(lax.axis_index("head"), sub)
    for k in range(sub):
        for h in range(heads):
            at = pl.ds(pl.multiple_of((me ^ k) * (heads * DK) + h * DK, DK), DK)
            core = pieces[k][:, h * DK : (h + 1) * DK].astype(f32)
            normed = core * lax.rsqrt(jnp.mean(core * core, axis=1, keepdims=True) + norm_eps)
            out_ref[0, :, at] = (normed * gain_ref[:, at] * jax.nn.sigmoid(gate_ref[0, :, at].astype(f32))).astype(bf16)


def product(a, b):
    return jnp.einsum("hij,hjk->hik", a, b, preferred_element_type=f32)


def before(span, *after):
    count = lax.axis_size("seq")
    place = lax.axis_index("seq")
    unit_mat = jnp.broadcast_to(jnp.eye(DK, dtype=bf16), span.shape[:1] + (DK, DK))
    raw = True
    early, whole = None, span
    size = 1
    while size < count:
        final = 2 * size >= count
        payload = whole[..., :DK] if final and size == 1 else whole
        got = None
        for t in range(size):
            pairs = [
                (base + size - 1, base + size + t)
                for base in range(0, count, 2 * size)
                if base + size + t < count
            ]
            part = lax.ppermute(payload, "seq", pairs)
            got = part if got is None else got + part
        if final:
            break
        right = (place // size) % 2 == 1
        if size == 1:
            early = got
        else:
            e_move = early[..., DK:]
            if raw:
                e_move = jnp.where(place % 2 == 1, e_move, unit_mat)
            raw = False
            moved = product(e_move, got)
            early = jnp.concatenate(
                [
                    (early[..., :DK].astype(f32) + moved[..., :DK]).astype(bf16),
                    jnp.where(right, moved[..., DK:].astype(bf16), e_move),
                ],
                axis=2,
            )
        share = whole.shape[0]
        last = 4 * size >= count
        whole = pl.pallas_call(
            functools.partial(relay_kernel, share),
            out_shape=jax.ShapeDtypeStruct((share, DK, DK if last else 2 * DK), bf16),
            in_specs=[VMEM] * 2 + [ANY] * len(after),
            out_specs=VMEM,
            compiler_params=params(16),
            cost_estimate=cost(0, 0),
            name=f"relay_{size}",
        )(whole, got, *after)
        size *= 2
    if early is None:
        early = jnp.concatenate([jnp.zeros_like(unit_mat), unit_mat], axis=2)
    return early, got, raw


def per_device(
    query_rows,
    key_rows,
    value_rows,
    beta_raw,
    gate_latent,
    gate_up,
    dt_bias,
    decay_log,
    boundary,
    modality,
    out_gate,
    norm_gain,
):
    places = lax.axis_size("head")
    batches, tok, columns = query_rows.shape
    sub = min(places, 4)
    outer = places // sub
    total_heads = columns // DK
    heads = total_heads // sub
    share = heads // outer
    width = heads * DK
    blocks = tok * sub // BLOCK
    sds = jax.ShapeDtypeStruct
    by_head_t = jnp.swapaxes(beta_raw, 1, 2)
    sets = ([(1, outer - 1)] if outer > 1 else []) + [(0, 1)]
    misc = tok // 16 + misc_rows(heads) // 16

    def pack_kv(of, first, shares, extras, *after):
        lanes = shares * share
        rows = 2 * tok * len(of) + (16 * -(-misc // lanes) if extras else 0)
        return pl.pallas_call(
            functools.partial(pack_kv_kernel, sub, outer, of, heads, first, extras),
            out_shape=[sds((rows, lanes * DK), bf16)] * sub,
            in_specs=[ANY] * (6 + len(after)),
            out_specs=[VMEM] * sub,
            scratch_shapes=[
                pltpu.VMEM(gate_latent.shape[1:], bf16),
                pltpu.VMEM(by_head_t.shape[1:], bf16),
                pltpu.VMEM(boundary.shape, jnp.int32),
                pltpu.VMEM(modality.shape, jnp.int32),
                pltpu.VMEM(by_head_t.shape[1:], f32),
                pltpu.SemaphoreType.DMA((sub, shares, 2 * len(of))),
                pltpu.SemaphoreType.DMA((4,)),
            ],
            compiler_params=params(16 if after else 60),
            cost_estimate=cost(0, 0),
            name=f"pack_kv_{of[0]}_{first}",
        )(key_rows, value_rows, gate_latent, by_head_t, boundary, modality, *after)

    hp = min(share, max(1, 8 // blocks))
    while share % hp:
        hp -= 1
    before_rows = max(1, blocks - 1)

    def by_head(*dims):
        return pl.BlockSpec((hp, *dims), lambda i: (i,) + (0,) * len(dims))

    per_head = by_head(blocks, DK, DK)
    wide_head = by_head(blocks, DK, 2 * DK)
    pre_head = by_head(before_rows, DK, DK)
    whole = pl.BlockSpec((blocks, BLOCK, BLOCK), lambda i: (0, 0, 0))
    levels = BLOCK.bit_length() - 1
    local_dims = [
        ((blocks, DK, DK), bf16),
        ((blocks, DK, DK), f32),
        ((blocks, DK, 2 * DK), bf16),
        ((blocks, DK, DK), f32),
        ((before_rows, DK, DK), f32),
        ((before_rows, DK, DK), bf16),
        ((DK, 2 * DK), bf16),
    ]
    count = lax.axis_size("head")

    def state_maps(b, part, *after):
        first, shares = sets[part]
        pieces = extras = kv[b]
        lane = sum(earlier for _, earlier in sets[:part]) * share * DK
        here = shares * share
        return pl.pallas_call(
            functools.partial(state_kernel, sub, outer, first, lane, blocks, heads, tok, hp),
            grid=(here // hp,),
            out_shape=[sds((here, *dims), kind) for dims, kind in local_dims] + [sds((blocks, BLOCK, BLOCK), f32)] * 2,
            in_specs=[SMEM] + [VMEM] * (2 * sub + 2) + [ANY] * len(after),
            out_specs=[by_head(*dims) for dims, _ in local_dims] + [whole, whole],
            scratch_shapes=[
                pltpu.VMEM((levels, BLOCK, BLOCK), bf16),
                pltpu.VMEM((blocks, BLOCK, BLOCK), f32),
                pltpu.VMEM((blocks, BLOCK, BLOCK), f32),
                pltpu.VMEM((blocks, misc_rows(heads), BLOCK), f32),
                pltpu.VMEM((blocks, BLOCK, BLOCK), bf16),
            ],
            compiler_params=params(),
            cost_estimate=cost(SCALE * here * blocks * 2e8, 0),
            name=f"state_maps_{b}_{first}",
        )(decay_log, *pieces, *extras, gate_up, dt_bias, *after)

    def swap(parts):
        return [parts[0]] + [
            lax.ppermute(parts[j], "head", [(i, i ^ (j * sub)) for i in range(count)]) for j in range(1, outer)
        ]

    def pack_q(*after):
        return pl.pallas_call(
            functools.partial(pack_q_kernel, sub, batches),
            out_shape=[sds((batches * tok, width), bf16)] * sub,
            in_specs=[ANY] * (1 + len(after)),
            out_specs=[VMEM] * sub,
            scratch_shapes=[pltpu.SemaphoreType.DMA((sub, batches))],
            compiler_params=params(16),
            cost_estimate=cost(0, 0),
            name="pack_q",
        )(query_rows, *after)

    def query_parts(b, part, *after):
        first, shares = sets[part]
        here = local[b][part]
        return pl.pallas_call(
            functools.partial(query_kernel, sub, outer, first, blocks, heads, tok, b, hp),
            grid=(shares * share // hp,),
            out_shape=[
                sds((shares * share, blocks, DK, DK), f32),
                sds((shares * share, blocks, DK, DK), bf16),
            ],
            in_specs=[VMEM] * sub + [per_head, per_head, wide_head, per_head] + [whole] * 2 + [ANY] * len(after),
            out_specs=[per_head] * 2,
            compiler_params=params(),
            cost_estimate=cost(SCALE * shares * share * blocks * 1e8, 0),
            name=f"query_parts_{b}_{first}",
        )(*q_here, *here[:4], *here[7:9], *after)

    def compose(b, parts, *after):
        return pl.pallas_call(
            functools.partial(compose_kernel, outer, share),
            out_shape=sds((share, DK, 2 * DK), bf16),
            in_specs=[VMEM] * outer + [ANY] * len(after),
            out_specs=VMEM,
            scratch_shapes=[pltpu.VMEM((outer, share, DK, 2 * DK), bf16)],
            compiler_params=params(),
            cost_estimate=cost(0, 0),
            name=f"compose_{b}",
        )(*parts, *after)

    def seeds(b, parts, early, incoming, raw, *after):
        return pl.pallas_call(
            functools.partial(seed_kernel, outer, share, raw),
            out_shape=[sds((share, DK, DK), bf16)] * outer,
            in_specs=[VMEM] * (outer + 2) + [ANY] * len(after),
            out_specs=[VMEM] * outer,
            scratch_shapes=[
                pltpu.VMEM((outer, share, DK, 2 * DK), bf16),
                pltpu.VMEM((outer, share, DK, DK), bf16),
            ],
            compiler_params=params(16),
            cost_estimate=cost(0, 0),
            name=f"seeds_{b}",
        )(*parts, early, incoming, *after)

    def outputs(b, queries, given):
        operands = []
        for made, here in zip(queries, local[b]):
            operands += [*made, *here[4:6]]
        return pl.pallas_call(
            functools.partial(output_kernel, sub, outer, sets, blocks, heads, tok),
            out_shape=[sds((tok, width), bf16)] * sub,
            in_specs=[VMEM] * (len(operands) + outer),
            out_specs=[VMEM] * sub,
            compiler_params=params(),
            cost_estimate=cost(SCALE * heads * blocks * 2e7, 0),
            name=f"span_outputs_{b}",
        )(*given, *operands)

    def swapped(made):
        sent = []
        if outer > 1:
            spans = made[0][6]
            sent = [spans] if outer == 2 else [spans[j * share : (j + 1) * share] for j in range(outer - 1)]
        return swap([made[-1][6]] + sent)

    parts_here = range(len(sets))
    jobs = [(b, part) for part in parts_here for b in range(batches)]
    local = [[None] * len(sets) for _ in range(batches)]
    queries = [[] for _ in range(batches)]
    moved, totals, begins, outs, back, relays = {}, {}, {}, {}, [], {}
    token = None
    kv = []
    for b in range(batches):
        packed = pack_kv([b], sets[0][0], outer, True, *([] if token is None else [token]))
        kv.append(exchange(packed))
        token = kv[b][-1]
    packed_q = pack_q(token)
    q_here = exchange(packed_q)
    token = packed[0]
    for b, part in jobs:
        local[b][part] = state_maps(b, part, token)
    for b in range(batches):
        moved[b] = swapped(local[b])
    def chain(b, *after):
        totals[b] = compose(b, moved[b], *after)
        relays[b] = before(totals[b])
        begins[b] = seeds(b, moved[b], *relays[b])

    last = batches - 1
    for part in parts_here:
        queries[last].append(query_parts(last, part))
    for b in range(batches):
        chain(b, *([made[1] for made in queries[last]] if b == last else []))
    for b in range(last):
        for part in parts_here:
            queries[b].append(query_parts(b, part))
    for b in range(batches):
        outs[b] = outputs(b, queries[b], swap(begins[b]))
        back.append(exchange(outs[b]))

    mixed = None
    for b in range(batches):
        rows = pl.BlockSpec((1, tok, columns), lambda i, b=b: (b, 0, 0))
        mixed = pl.pallas_call(
            functools.partial(finish_kernel, sub, heads),
            grid=(1,),
            out_shape=sds((batches, tok, columns), bf16),
            in_specs=[pl.BlockSpec((tok, width), lambda i: (0, 0))] * sub
            + [rows, pl.BlockSpec((1, columns), lambda i: (0, 0))]
            + ([] if b == 0 else [ANY]),
            out_specs=rows,
            input_output_aliases={} if b == 0 else {sub + 2: 0},
            compiler_params=params(),
            cost_estimate=cost(0, 0),
            name=f"finish_{b}",
        )(*back[b], out_gate, norm_gain[None, :], *([] if b == 0 else [mixed]))
    return mixed


def solution(mesh):
    return jax.shard_map(
        per_device,
        mesh=mesh,
        in_specs=(
            P(None, ("seq", "head"), None),
            P(None, ("seq", "head"), None),
            P(None, ("seq", "head"), None),
            P(None, ("seq", "head"), None),
            P(None, ("seq", "head"), None),
            P(),
            P(),
            P(),
            P(None, ("seq", "head")),
            P(None, ("seq", "head")),
            P(None, ("seq", "head"), None),
            P(),
        ),
        out_specs=P(None, ("seq", "head"), None),
        check_vma=False,
    )
```

```python
import functools

import jax
import jax.numpy as jnp
from jax import lax
from jax.experimental import pallas as pl
from jax.experimental.pallas import tpu as pltpu
from jax.sharding import PartitionSpec as P

DK = 128
BLOCK = 128
norm_eps = 1e-06
LOG2E = 1.4426950408889634
f32 = jnp.float32
bf16 = jnp.bfloat16
ANY = pl.BlockSpec(memory_space=pl.ANY)
VMEM = pl.BlockSpec(memory_space=pltpu.VMEM)
SMEM = pl.BlockSpec(memory_space=pltpu.SMEM)
SCALE = 0.1


def params(mib=48):
    return pltpu.CompilerParams(vmem_limit_bytes=mib * 1024 * 1024)


def misc_rows(heads):
    return -(-(heads + 2) // 16) * 16


def cost(flops, nbytes):
    return pl.CostEstimate(flops=int(flops), bytes_accessed=int(nbytes), transcendentals=0)


def dot(a, b, dims=((1,), (0,))):
    return lax.dot_general(
        a.astype(bf16), b.astype(bf16), (dims, ((), ())), preferred_element_type=f32
    )


def split(a):
    high = a.astype(bf16)
    return high, (a - high.astype(f32)).astype(bf16)


def dot3(a, b, dims=((1,), (0,))):
    ah, al = split(a)
    bh, bl = split(b)
    return dot(ah, bh, dims) + (dot(ah, bl, dims) + dot(al, bh, dims))


NT = ((1,), (1,))


def pack_kv_kernel(sub, ways, outer, batches, heads, first, extras, key_ref, value_ref, latent_ref, beta_ref, mark_ref, kind_ref, *rest):
    outs, (latent, beta, mark, kind, wide, sem, small_sem) = rest[-len(ways) - 7 : -7], rest[-7:]
    lo = lax.rem(lax.axis_index("head"), sub)
    hi = lax.div(lax.axis_index("head"), sub)
    rows, width = key_ref.shape[1], outs[0].shape[1]
    part = heads // outer * DK
    copies = []
    for place_out, k in enumerate(ways):
        for j in range(width // part):
            col = pl.multiple_of(((lo ^ k) * outer + (hi ^ ((first + j) % outer))) * part, part)
            for n, batch in enumerate(batches):
                for i, ref in enumerate((key_ref, value_ref)):
                    copies.append(
                        pltpu.make_async_copy(
                            ref.at[batch, :, pl.ds(col, part)],
                            outs[place_out].at[pl.ds((2 * n + i) * rows, rows), pl.ds(j * part, part)],
                            sem.at[place_out, j, 2 * n + i],
                        )
                    )
                    copies[-1].start()
    if extras:
        (batch,) = batches
        small = [
            pltpu.make_async_copy(source, target, small_sem.at[i])
            for i, (source, target) in enumerate(
                ((latent_ref.at[batch], latent), (beta_ref.at[batch], beta), (mark_ref, mark), (kind_ref, kind))
            )
        ]
        for c in small:
            c.start()
        for c in small:
            c.wait()
        lanes = width // 128
        misc = misc_rows(heads)
        wide[...] = beta[...].astype(f32)
        tokens = jnp.concatenate([mark[batch : batch + 1].astype(f32), kind[batch : batch + 1].astype(f32)], axis=0)
        for place_out, k in enumerate(ways):
            own = wide[pl.ds(pl.multiple_of((lo ^ k) * heads, heads), heads), :]
            values = jnp.concatenate([own, tokens, jnp.zeros((misc - heads - 2, rows), f32)], axis=0)
            values = jnp.concatenate([values, jnp.zeros((misc, 128 - rows), f32)], axis=1).astype(bf16)
            chunks = [latent[16 * j : 16 * j + 16] for j in range(rows // 16)]
            chunks += [values[16 * j : 16 * j + 16] for j in range(misc // 16)]
            chunks += [jnp.zeros((16, 128), bf16)] * (-len(chunks) % lanes)
            for c, chunk in enumerate(chunks):
                at = 2 * rows + 16 * (c // lanes)
                outs[place_out][at : at + 16, (c % lanes) * 128 : (c % lanes + 1) * 128] = chunk
    for c in copies:
        c.wait()


def pack_q_kernel(sub, batches, query_ref, *rest):
    outs, sem = rest[-sub - 1 : -1], rest[-1]
    lo = lax.rem(lax.axis_index("head"), sub)
    rows, width = query_ref.shape[1], query_ref.shape[2] // sub
    copies = []
    for k in range(sub):
        col = pl.multiple_of((lo ^ k) * width, width)
        for b in range(batches):
            copies.append(
                pltpu.make_async_copy(
                    query_ref.at[b, :, pl.ds(col, width)], outs[k].at[pl.ds(b * rows, rows)], sem.at[k, b]
                )
            )
            copies[-1].start()
    for c in copies:
        c.wait()


def exchange(pieces):
    count = lax.axis_size("head")
    got = {
        k: lax.ppermute(pieces[k], "head", [(i, i ^ k) for i in range(count)]) for k in range(len(pieces) - 1, 0, -1)
    }
    return [pieces[0]] + [got[k] for k in range(1, len(pieces))]


def place(outer, first, share, hp):
    at = pl.program_id(0) * hp
    hi = lax.div(lax.axis_index("head"), lax.axis_size("head") // outer)
    return (hi ^ (first + lax.div(at, share))) * share + lax.rem(at, share)


def reorder(parts, place, bits):
    for bit in range(bits):
        flipped = lax.rem(lax.div(place, 2**bit), 2) == 1
        parts = [jnp.where(flipped, parts[i ^ 2**bit], parts[i]) for i in range(len(parts))]
    return parts


def token_rows(pieces, slot, lo, tok, load):
    per = BLOCK // tok
    parts = [load(pieces[slot * per + r]) for r in range(per)]
    return jnp.concatenate(reorder(parts, lax.rem(lo, per), per.bit_length() - 1), axis=0)


def state_kernel(sub, outer, first, lane, blocks, heads, tok, hp, decay_ref, *rest):
    pieces, extras = rest[:sub], rest[sub : 2 * sub]
    up_ref, bias_ref = rest[2 * sub : 2 * sub + 2]
    w_ref, u_ref, shrink_ref, growth_ref, opre_ref, mpre_ref, span_ref, mask_ref, alive_ref = rest[-14:-5]
    levels, kinds, lasts, values, gates = rest[-5:]
    me = lax.rem(lax.axis_index("head"), sub)
    start = place(outer, first, heads // outer, hp)
    width = heads * DK
    per = BLOCK // tok
    row = lax.broadcasted_iota(jnp.int32, (BLOCK, BLOCK), 0)
    col = lax.broadcasted_iota(jnp.int32, (BLOCK, BLOCK), 1)
    low = (row >= col).astype(f32)
    low_b = low.astype(bf16)
    up_b = (row <= col).astype(bf16)
    unit_mat = (row == col).astype(bf16)
    count = BLOCK.bit_length() - 1
    step = pl.program_id(0)

    @pl.when(step == 0)
    def _():
        for level in range(count):
            size = 2**level
            here = (row // size == col // size + 1) & ((row // size) % 2 == 1)
            levels[level] = here.astype(bf16)
        lanes = extras[0].shape[1] // 128
        misc = misc_rows(heads)

        def chunk(piece, c):
            at = 2 * tok + 16 * (c // lanes)
            return piece[at : at + 16, (c % lanes) * 128 : (c % lanes + 1) * 128]

        for n in range(blocks):
            parts = [
                jnp.concatenate(
                    [chunk(extras[n * per + r], tok // 16 + j).astype(f32) for j in range(misc // 16)], axis=0
                )[:, :tok]
                for r in range(per)
            ]
            tall = jnp.concatenate(reorder(parts, lax.rem(me, per), per.bit_length() - 1), axis=1)
            values[n] = jax.nn.sigmoid(tall)
            mark = tall[heads : heads + 1]
            two = jnp.transpose(jnp.concatenate([tall[heads : heads + 2], jnp.zeros((6, BLOCK), f32)], axis=0))
            own = dot(low_b, jnp.broadcast_to(two[:, 0:1], (BLOCK, BLOCK)))
            other = dot(jnp.broadcast_to(mark, (BLOCK, BLOCK)), up_b)
            mask_ref[n] = jnp.where(own == other, low, 0.0)
            alive_ref[n] = (own == 0).astype(f32)
            lasts[n] = (own == other[:, BLOCK - 1 : BLOCK]).astype(f32)
            kinds[n] = jnp.broadcast_to(two[:, 1:2], (BLOCK, BLOCK))
            gates[n] = token_rows(
                extras, n, me, tok, lambda p: jnp.concatenate([chunk(p, j) for j in range(tok // 16)], axis=0)
            )

    low2 = jnp.concatenate([low_b, low_b], axis=1)
    lower = (row > col).astype(f32)
    items = [(i, n) for i in range(hp) for n in range(blocks)]
    every = range(blocks)
    strict_all, rhs_all, tail_all, carry_all = {}, {}, {}, {}
    betas = []
    for n in range(blocks):
        mine = values[n, pl.ds(start, hp), :]
        betas.append(jnp.transpose(jnp.concatenate([mine, jnp.zeros((8 - hp % 8, BLOCK), f32)], axis=0)))
    for i in range(hp):
        h = start + i
        at = pl.ds(pl.multiple_of(lane + (step * hp + i) * DK, DK), DK)
        bias_at = pl.ds(pl.multiple_of(me * width + h * DK, DK), DK)
        audio, text = bias_ref[0:1, bias_at], bias_ref[1:2, bias_at]
        rate = -LOG2E * jnp.exp(jnp.full((1, DK), decay_ref[me * heads + h], f32))
        for n in range(blocks):
            gate = dot(gates[n], up_ref[:, bias_at]).astype(bf16).astype(f32)
            pre = gate + jnp.where(kinds[n] == 1.0, text, audio)
            soft = jnp.maximum(pre, 0.0) + jnp.log(1.0 + jnp.exp(-jnp.abs(pre)))
            high, rest_part = split(rate * soft)
            total = dot(low2, jnp.concatenate([high, rest_part], axis=0))
            key = token_rows(pieces, n, me, tok, lambda p: p[0:tok, at]).astype(f32)
            value = token_rows(pieces, n, me, tok, lambda p: p[tok : 2 * tok, at]).astype(f32)
            unit = key * lax.rsqrt(jnp.sum(key * key, axis=1, keepdims=True) + norm_eps)
            growth = jnp.exp2(total)
            grown = unit * growth
            shrunk, shrunk_rest = split(unit * jnp.exp2(-total))
            last = total[BLOCK - 1 : BLOCK]
            tail = unit * (jnp.exp2(last - total) * lasts[n])
            carry = jnp.exp2(last) * alive_ref[n, BLOCK - 1 : BLOCK]
            beta = jnp.broadcast_to(betas[n][:, i : i + 1], (BLOCK, BLOCK))
            growth_ref[i, n] = growth
            shrink_ref[i, n, :, :DK] = shrunk
            shrink_ref[i, n, :, DK:] = shrunk_rest
            gram = dot(grown, shrunk, NT)
            strict_all[i, n] = (gram * (mask_ref[n] * lower) * beta).astype(bf16)
            rhs_all[i, n] = jnp.concatenate([beta * grown * alive_ref[n], beta * value], axis=1)
            tail_all[i, n] = jnp.transpose(tail)
            carry_all[i, n] = carry
    turned = jnp.transpose(jnp.concatenate([carry_all[t] for t in items] + [jnp.zeros((BLOCK - len(items), DK), f32)]))
    carry_all = {t: turned[:, j : j + 1] for j, t in enumerate(items)}
    inv = {t: unit_mat - strict_all[t] * levels[0] for t in items}
    for level in range(1, count):
        size = 2**level
        corner = {t: strict_all[t] * levels[level] for t in items}
        if size < 16:
            turn = {t: dot(inv[t], corner[t]) for t in items}
            inv = {t: inv[t] - dot(turn[t], inv[t]).astype(bf16) for t in items}
        else:
            pairs = BLOCK // (2 * size)
            four = {t: inv[t].reshape(pairs, 2, size, BLOCK) for t in items}
            odd = {t: four[t][:, 1].reshape(BLOCK // 2, BLOCK) for t in items}
            turn = {t: dot(odd[t], corner[t]) for t in items}
            odd = {t: odd[t] - dot(turn[t], inv[t]).astype(bf16) for t in items}
            inv = {
                t: jnp.stack([four[t][:, 0], odd[t].reshape(pairs, size, BLOCK)], axis=1).reshape(BLOCK, BLOCK)
                for t in items
            }
    both = {t: rhs_all[t] + dot(inv[t] - unit_mat, rhs_all[t]) for t in items}
    fade, offs = {}, {}
    for t in items:
        i, n = t
        w = both[t][:, :DK].astype(bf16)
        w_ref[i, n] = w
        u_ref[i, n] = both[t][:, DK:]
        uh, ul = split(both[t][:, DK:])
        th, tl = split(tail_all[t])
        joint = dot(th, jnp.concatenate([w, uh], axis=1))
        fade[t] = joint[:, :DK].astype(bf16)
        offs[t] = joint[:, DK:] + dot(jnp.concatenate([th, tl], axis=1), jnp.concatenate([ul, uh], axis=0))
    bits = blocks.bit_length() - 1
    for i in range(hp):
        for made in (fade, offs, carry_all):
            in_time = reorder([made[i, n] for n in every], lax.div(me, per), bits)
            for n in every:
                made[i, n] = in_time[n]
    offset = {i: offs[i, 0] for i in range(hp)}
    move = {i: jnp.where(row == col, carry_all[i, 0], 0.0) - fade[i, 0].astype(f32) for i in range(hp)}
    for n in range(1, blocks):
        for i in range(hp):
            opre_ref[i, n - 1] = offset[i]
            mpre_ref[i, n - 1] = move[i].astype(bf16)
            joint = dot(fade[i, n], jnp.concatenate([offset[i], move[i]], axis=1))
            offset[i] = carry_all[i, n] * offset[i] + offs[i, n] - joint[:, :DK]
            move[i] = carry_all[i, n] * move[i] - joint[:, DK:]
    for i in range(hp):
        span_ref[i] = jnp.concatenate([offset[i], move[i]], axis=1).astype(bf16)


def joined(later, earlier):
    both = dot(later[1], jnp.concatenate([earlier[0], earlier[1]], axis=1))
    return (later[0].astype(f32) + both[:, :DK]).astype(bf16), both[:, DK:].astype(bf16)


def ordered(outer, parts, order):
    hi = lax.div(lax.axis_index("head"), lax.axis_size("head") // outer)
    for j in range(outer):
        order[hi ^ j] = parts[j][...]


def compose_kernel(outer, share, *rest):
    parts, out_ref, order = rest[:outer], rest[-2], rest[-1]
    ordered(outer, parts, order)
    for h in range(share):
        whole = (order[0, h, :, :DK], order[0, h, :, DK:])
        for o in range(1, outer):
            whole = joined((order[o, h, :, :DK], order[o, h, :, DK:]), whole)
        out_ref[h, :, :DK] = whole[0]
        out_ref[h, :, DK:] = whole[1]


def relay_kernel(share, whole_ref, got_ref, *rest):
    out_ref = rest[-1]
    for h in range(share):
        whole = joined(
            (whole_ref[h, :, :DK], whole_ref[h, :, DK:]), (got_ref[h, :, :DK], got_ref[h, :, DK:])
        )
        out_ref[h, :, :DK] = whole[0]
        if out_ref.shape[2] > DK:
            out_ref[h, :, DK:] = whole[1]


def seed_kernel(outer, share, raw, *rest):
    parts = rest[:outer]
    early_ref, in_ref = rest[outer : outer + 2]
    outs, (order, seeds) = rest[-outer - 2 : -2], rest[-2:]
    hi = lax.div(lax.axis_index("head"), lax.axis_size("head") // outer)
    ordered(outer, parts, order)
    row = lax.broadcasted_iota(jnp.int32, (DK, DK), 0)
    col = lax.broadcasted_iota(jnp.int32, (DK, DK), 1)
    odd = lax.rem(lax.axis_index("seq"), 2) == 1
    for h in range(share):
        incoming = in_ref[h]
        through = dot(early_ref[h, :, DK:], incoming)
        if raw:
            through = jnp.where(odd, through, incoming.astype(f32))
        state = (early_ref[h, :, :DK].astype(f32) + through).astype(bf16)
        seeds[0, h] = state
        for o in range(1, outer):
            moved = dot(order[o - 1, h, :, DK:], state)
            state = (order[o - 1, h, :, :DK].astype(f32) + moved).astype(bf16)
            seeds[o, h] = state
    for j in range(outer):
        outs[j][...] = seeds[hi ^ j]


def query_kernel(sub, outer, first, blocks, heads, tok, batch, hp, *rest):
    pieces = rest[:sub]
    w_ref, u_ref, shrink_ref, growth_ref, mask_ref, alive_ref = rest[sub : sub + 6]
    base_ref, rows_ref = rest[-2:]
    lo = lax.rem(lax.axis_index("head"), sub)
    items = [(i, n) for i in range(hp) for n in range(blocks)]
    start = place(outer, first, heads // outer, hp)
    at = [pl.ds(pl.multiple_of((start + i) * DK, DK), DK) for i in range(hp)]
    grown, mix = {}, {}
    for i, n in items:
        query = token_rows(pieces, n, lo, tok, lambda p: p[batch * tok : (batch + 1) * tok, at[i]]).astype(f32)
        unit = query * (lax.rsqrt(jnp.sum(query * query, axis=1, keepdims=True) + norm_eps) * DK ** (-0.5))
        grown[i, n] = unit * growth_ref[i, n]
        gh, gl = split(grown[i, n])
        shrunk = shrink_ref[i, n]
        mix[i, n] = mask_ref[n] * dot(
            jnp.concatenate([gh, gh, gl], axis=1), jnp.concatenate([shrunk, shrunk[:, :DK]], axis=1), NT
        )
    for i, n in items:
        mh, ml = split(mix[i, n])
        uh, ul = split(u_ref[i, n])
        both = dot(mh, jnp.concatenate([uh, w_ref[i, n]], axis=1))
        rest_part = dot(jnp.concatenate([mh, ml], axis=1), jnp.concatenate([ul, uh], axis=0))
        base_ref[i, n] = both[:, :DK] + rest_part
        rows_ref[i, n] = (grown[i, n] * alive_ref[n] - both[:, DK:]).astype(bf16)


def output_kernel(sub, outer, sets, blocks, heads, tok, slots, *rest):
    seeds, rest = rest[:outer], rest[outer:]
    per = BLOCK // tok
    outs = rest[-len(slots) * per :]
    lo = lax.rem(lax.axis_index("head"), sub)
    hi = lax.div(lax.axis_index("head"), sub)
    share = heads // outer
    for part, (first, shares) in enumerate(sets):
        base_ref, rows_ref, opre_ref, mpre_ref = rest[4 * part : 4 * part + 4]
        for r in range(shares * share):
            j, i = first + r // share, r % share
            at = pl.ds(pl.multiple_of(((hi ^ j) * share + i) * DK, DK), DK)
            seed = seeds[j][i]
            states = [seed] + [
                (opre_ref[r, n] + dot(mpre_ref[r, n], seed)).astype(bf16) for n in range(blocks - 1)
            ]
            states = reorder(states, lax.div(lo, per), blocks.bit_length() - 1)
            for m, n in enumerate(slots):
                core = (base_ref[r, n] + dot(rows_ref[r, n], states[n])).astype(bf16)
                rows = reorder([core[t * tok : (t + 1) * tok] for t in range(per)], lax.rem(lo, per), per.bit_length() - 1)
                for t in range(per):
                    outs[m * per + t][:, at] = rows[t]


def finish_kernel(sub, heads, *rest):
    pieces = rest[:sub]
    gate_ref, gain_ref = rest[sub : sub + 2]
    out_ref = rest[-1]
    me = lax.rem(lax.axis_index("head"), sub)
    for k in range(sub):
        for h in range(heads):
            at = pl.ds(pl.multiple_of((me ^ k) * (heads * DK) + h * DK, DK), DK)
            core = pieces[k][:, h * DK : (h + 1) * DK].astype(f32)
            normed = core * lax.rsqrt(jnp.mean(core * core, axis=1, keepdims=True) + norm_eps)
            out_ref[0, :, at] = (normed * gain_ref[:, at] * jax.nn.sigmoid(gate_ref[0, :, at].astype(f32))).astype(bf16)


def product(a, b):
    return jnp.einsum("hij,hjk->hik", a, b, preferred_element_type=f32)


def before(span, *after):
    count = lax.axis_size("seq")
    place = lax.axis_index("seq")
    unit_mat = jnp.broadcast_to(jnp.eye(DK, dtype=bf16), span.shape[:1] + (DK, DK))
    raw = True
    early, whole = None, span
    size = 1
    while size < count:
        final = 2 * size >= count
        payload = whole[..., :DK] if final and size == 1 else whole
        got = None
        for t in range(size):
            pairs = [
                (base + size - 1, base + size + t)
                for base in range(0, count, 2 * size)
                if base + size + t < count
            ]
            part = lax.ppermute(payload, "seq", pairs)
            got = part if got is None else got + part
        if final:
            break
        right = (place // size) % 2 == 1
        if size == 1:
            early = got
        else:
            e_move = early[..., DK:]
            if raw:
                e_move = jnp.where(place % 2 == 1, e_move, unit_mat)
            raw = False
            moved = product(e_move, got)
            early = jnp.concatenate(
                [
                    (early[..., :DK].astype(f32) + moved[..., :DK]).astype(bf16),
                    jnp.where(right, moved[..., DK:].astype(bf16), e_move),
                ],
                axis=2,
            )
        share = whole.shape[0]
        last = 4 * size >= count
        whole = pl.pallas_call(
            functools.partial(relay_kernel, share),
            out_shape=jax.ShapeDtypeStruct((share, DK, DK if last else 2 * DK), bf16),
            in_specs=[VMEM] * 2 + [ANY] * len(after),
            out_specs=VMEM,
            compiler_params=params(16),
            cost_estimate=cost(0, 0),
            name=f"relay_{size}",
        )(whole, got, *after)
        size *= 2
    if early is None:
        early = jnp.concatenate([jnp.zeros_like(unit_mat), unit_mat], axis=2)
    return early, got, raw


def per_device(
    query_rows,
    key_rows,
    value_rows,
    beta_raw,
    gate_latent,
    gate_up,
    dt_bias,
    decay_log,
    boundary,
    modality,
    out_gate,
    norm_gain,
):
    places = lax.axis_size("head")
    batches, tok, columns = query_rows.shape
    sub = min(places, 4)
    outer = places // sub
    total_heads = columns // DK
    heads = total_heads // sub
    share = heads // outer
    width = heads * DK
    blocks = tok * sub // BLOCK
    sds = jax.ShapeDtypeStruct
    by_head_t = jnp.swapaxes(beta_raw, 1, 2)
    sets = ([(1, outer - 1)] if outer > 1 else []) + [(0, 1)]
    misc = tok // 16 + misc_rows(heads) // 16

    def pack_kv(of, first, shares, extras, ways, direct, *after):
        lanes = shares * share
        rows = 2 * tok * len(of) + (16 * -(-misc // lanes) if extras else 0)
        return pl.pallas_call(
            functools.partial(pack_kv_kernel, sub, ways, outer, of, heads, first, extras),
            out_shape=[sds((rows, lanes * DK), bf16)] * len(ways),
            in_specs=[ANY] * (6 + len(after)),
            out_specs=[VMEM] * len(ways),
            scratch_shapes=[
                pltpu.VMEM(gate_latent.shape[1:], bf16),
                pltpu.VMEM(by_head_t.shape[1:], bf16),
                pltpu.VMEM(boundary.shape, jnp.int32),
                pltpu.VMEM(modality.shape, jnp.int32),
                pltpu.VMEM(by_head_t.shape[1:], f32),
                pltpu.SemaphoreType.DMA((len(ways), shares, 2 * len(of))),
                pltpu.SemaphoreType.DMA((4,)),
            ],
            compiler_params=params(60 if direct else 16),
            cost_estimate=cost(0, 0),
            name=f"pack_kv_{of[0]}_{ways[0]}",
        )(key_rows, value_rows, gate_latent, by_head_t, boundary, modality, *after)

    hp = min(share, max(1, 8 // blocks))
    while share % hp:
        hp -= 1
    before_rows = max(1, blocks - 1)

    def by_head(*dims):
        return pl.BlockSpec((hp, *dims), lambda i: (i,) + (0,) * len(dims))

    per_head = by_head(blocks, DK, DK)
    wide_head = by_head(blocks, DK, 2 * DK)
    pre_head = by_head(before_rows, DK, DK)
    whole = pl.BlockSpec((blocks, BLOCK, BLOCK), lambda i: (0, 0, 0))
    levels = BLOCK.bit_length() - 1
    local_dims = [
        ((blocks, DK, DK), bf16),
        ((blocks, DK, DK), f32),
        ((blocks, DK, 2 * DK), bf16),
        ((blocks, DK, DK), f32),
        ((before_rows, DK, DK), f32),
        ((before_rows, DK, DK), bf16),
        ((DK, 2 * DK), bf16),
    ]
    count = lax.axis_size("head")

    def state_maps(b, part, *after):
        first, shares = sets[part]
        pieces = extras = kv[b]
        lane = sum(earlier for _, earlier in sets[:part]) * share * DK
        here = shares * share
        return pl.pallas_call(
            functools.partial(state_kernel, sub, outer, first, lane, blocks, heads, tok, hp),
            grid=(here // hp,),
            out_shape=[sds((here, *dims), kind) for dims, kind in local_dims] + [sds((blocks, BLOCK, BLOCK), f32)] * 2,
            in_specs=[SMEM] + [VMEM] * (2 * sub + 2) + [ANY] * len(after),
            out_specs=[by_head(*dims) for dims, _ in local_dims] + [whole, whole],
            scratch_shapes=[
                pltpu.VMEM((levels, BLOCK, BLOCK), bf16),
                pltpu.VMEM((blocks, BLOCK, BLOCK), f32),
                pltpu.VMEM((blocks, BLOCK, BLOCK), f32),
                pltpu.VMEM((blocks, misc_rows(heads), BLOCK), f32),
                pltpu.VMEM((blocks, BLOCK, BLOCK), bf16),
            ],
            compiler_params=params(),
            cost_estimate=cost(SCALE * here * blocks * 2e8, 0),
            name=f"state_maps_{b}_{first}",
        )(decay_log, *pieces, *extras, gate_up, dt_bias, *after)

    def swap(parts):
        return [parts[0]] + [
            lax.ppermute(parts[j], "head", [(i, i ^ (j * sub)) for i in range(count)]) for j in range(1, outer)
        ]

    def pack_q(*after):
        return pl.pallas_call(
            functools.partial(pack_q_kernel, sub, batches),
            out_shape=[sds((batches * tok, width), bf16)] * sub,
            in_specs=[ANY] * (1 + len(after)),
            out_specs=[VMEM] * sub,
            scratch_shapes=[pltpu.SemaphoreType.DMA((sub, batches))],
            compiler_params=params(16),
            cost_estimate=cost(0, 0),
            name="pack_q",
        )(query_rows, *after)

    def query_parts(b, part, *after):
        first, shares = sets[part]
        here = local[b][part]
        return pl.pallas_call(
            functools.partial(query_kernel, sub, outer, first, blocks, heads, tok, b, hp),
            grid=(shares * share // hp,),
            out_shape=[
                sds((shares * share, blocks, DK, DK), f32),
                sds((shares * share, blocks, DK, DK), bf16),
            ],
            in_specs=[VMEM] * sub + [per_head, per_head, wide_head, per_head] + [whole] * 2 + [ANY] * len(after),
            out_specs=[per_head] * 2,
            compiler_params=params(),
            cost_estimate=cost(SCALE * shares * share * blocks * 1e8, 0),
            name=f"query_parts_{b}_{first}",
        )(*q_here, *here[:4], *here[7:9], *after)

    def compose(b, parts, *after):
        return pl.pallas_call(
            functools.partial(compose_kernel, outer, share),
            out_shape=sds((share, DK, 2 * DK), bf16),
            in_specs=[VMEM] * outer + [ANY] * len(after),
            out_specs=VMEM,
            scratch_shapes=[pltpu.VMEM((outer, share, DK, 2 * DK), bf16)],
            compiler_params=params(),
            cost_estimate=cost(0, 0),
            name=f"compose_{b}",
        )(*parts, *after)

    def seeds(b, parts, early, incoming, raw, *after):
        return pl.pallas_call(
            functools.partial(seed_kernel, outer, share, raw),
            out_shape=[sds((share, DK, DK), bf16)] * outer,
            in_specs=[VMEM] * (outer + 2) + [ANY] * len(after),
            out_specs=[VMEM] * outer,
            scratch_shapes=[
                pltpu.VMEM((outer, share, DK, 2 * DK), bf16),
                pltpu.VMEM((outer, share, DK, DK), bf16),
            ],
            compiler_params=params(16),
            cost_estimate=cost(0, 0),
            name=f"seeds_{b}",
        )(*parts, early, incoming, *after)

    def outputs(b, queries, given):
        operands = []
        for made, here in zip(queries, local[b]):
            operands += [*made, *here[4:6]]
        pieces = {}
        per = sub // blocks
        near = (blocks + 1) // 2
        after = []
        for slots in (list(range(near, blocks)), list(range(near))):
            if not slots:
                continue
            made = pl.pallas_call(
                functools.partial(output_kernel, sub, outer, sets, blocks, heads, tok, slots),
                out_shape=[sds((tok, width), bf16)] * (len(slots) * per),
                in_specs=[VMEM] * (len(operands) + outer) + [ANY] * len(after),
                out_specs=[VMEM] * (len(slots) * per),
                compiler_params=params(),
                cost_estimate=cost(SCALE * heads * len(slots) * 2e7, 0),
                name=f"span_outputs_{b}_{slots[0]}",
            )(*given, *operands, *after)
            after = [made[0]]
            for m, n in enumerate(slots):
                for t in range(per):
                    pieces[n * per + t] = made[m * per + t]
        return [pieces[k] for k in range(sub)]

    def swapped(made):
        sent = []
        if outer > 1:
            spans = made[0][6]
            sent = [spans] if outer == 2 else [spans[j * share : (j + 1) * share] for j in range(outer - 1)]
        return swap([made[-1][6]] + sent)

    parts_here = range(len(sets))
    jobs = [(b, part) for part in parts_here for b in range(batches)]
    local = [[None] * len(sets) for _ in range(batches)]
    queries = [[] for _ in range(batches)]
    moved, totals, begins, outs, back, relays = {}, {}, {}, {}, [], {}
    token = None
    kv = []
    for b in range(batches):
        if b == 0:
            far = pack_kv([b], sets[0][0], outer, True, [sub - 1], True)
            packed = pack_kv([b], sets[0][0], outer, True, list(range(sub - 1)), True, far[0]) + far if sub > 1 else far
        else:
            packed = pack_kv([b], sets[0][0], outer, True, list(range(sub)), False, token)
        kv.append(exchange(packed))
        token = kv[b][-1]
    packed_q = pack_q(token)
    q_here = exchange(packed_q)
    token = packed[0]
    for b, part in jobs:
        local[b][part] = state_maps(b, part, token)
    for b in range(batches):
        moved[b] = swapped(local[b])
    def chain(b, *after):
        totals[b] = compose(b, moved[b], *after)
        relays[b] = before(totals[b])
        begins[b] = seeds(b, moved[b], *relays[b])

    last = batches - 1
    for part in parts_here:
        queries[last].append(query_parts(last, part))
    for b in range(batches):
        chain(b, *([made[1] for made in queries[last]] if b == last else []))
    for b in range(last):
        for part in parts_here:
            queries[b].append(query_parts(b, part))
    for b in range(batches):
        outs[b] = outputs(b, queries[b], swap(begins[b]))
        back.append(exchange(outs[b]))

    mixed = None
    for b in range(batches):
        rows = pl.BlockSpec((1, tok, columns), lambda i, b=b: (b, 0, 0))
        mixed = pl.pallas_call(
            functools.partial(finish_kernel, sub, heads),
            grid=(1,),
            out_shape=sds((batches, tok, columns), bf16),
            in_specs=[pl.BlockSpec((tok, width), lambda i: (0, 0))] * sub
            + [rows, pl.BlockSpec((1, columns), lambda i: (0, 0))]
            + ([] if b == 0 else [ANY]),
            out_specs=rows,
            input_output_aliases={} if b == 0 else {sub + 2: 0},
            compiler_params=params(),
            cost_estimate=cost(0, 0),
            name=f"finish_{b}",
        )(*back[b], out_gate, norm_gain[None, :], *([] if b == 0 else [mixed]))
    return mixed


def solution(mesh):
    return jax.shard_map(
        per_device,
        mesh=mesh,
        in_specs=(
            P(None, ("seq", "head"), None),
            P(None, ("seq", "head"), None),
            P(None, ("seq", "head"), None),
            P(None, ("seq", "head"), None),
            P(None, ("seq", "head"), None),
            P(),
            P(),
            P(),
            P(None, ("seq", "head")),
            P(None, ("seq", "head")),
            P(None, ("seq", "head"), None),
            P(),
        ),
        out_specs=P(None, ("seq", "head"), None),
        check_vma=False,
    )
```

```python
import functools

import jax
import jax.numpy as jnp
from jax import lax
from jax.experimental import pallas as pl
from jax.experimental.pallas import tpu as pltpu
from jax.sharding import PartitionSpec as P

DK = 128
BLOCK = 128
norm_eps = 1e-06
LOG2E = 1.4426950408889634
f32 = jnp.float32
bf16 = jnp.bfloat16
ANY = pl.BlockSpec(memory_space=pl.ANY)
VMEM = pl.BlockSpec(memory_space=pltpu.VMEM)
SMEM = pl.BlockSpec(memory_space=pltpu.SMEM)
SCALE = 0.1


def params(mib=48):
    return pltpu.CompilerParams(vmem_limit_bytes=mib * 1024 * 1024)


def misc_rows(heads):
    return -(-(heads + 2) // 16) * 16


def cost(flops, nbytes):
    return pl.CostEstimate(flops=int(flops), bytes_accessed=int(nbytes), transcendentals=0)


def dot(a, b, dims=((1,), (0,))):
    return lax.dot_general(
        a.astype(bf16), b.astype(bf16), (dims, ((), ())), preferred_element_type=f32
    )


def split(a):
    high = a.astype(bf16)
    return high, (a - high.astype(f32)).astype(bf16)


def dot3(a, b, dims=((1,), (0,))):
    ah, al = split(a)
    bh, bl = split(b)
    return dot(ah, bh, dims) + (dot(ah, bl, dims) + dot(al, bh, dims))


NT = ((1,), (1,))


def pack_kv_kernel(sub, ways, outer, batches, heads, first, extras, key_ref, value_ref, latent_ref, beta_ref, mark_ref, kind_ref, *rest):
    outs, (latent, beta, mark, kind, wide, sem, small_sem) = rest[-len(ways) - 7 : -7], rest[-7:]
    lo = lax.rem(lax.axis_index("head"), sub)
    hi = lax.div(lax.axis_index("head"), sub)
    rows, width = key_ref.shape[1], outs[0].shape[1]
    part = heads // outer * DK
    copies = []
    cuts = sem.shape[3]
    for place_out, k in enumerate(ways):
        for j in range(width // part):
            col = pl.multiple_of(((lo ^ k) * outer + (hi ^ ((first + j) % outer))) * part, part)
            for n, batch in enumerate(batches):
                for i, ref in enumerate((key_ref, value_ref)):
                    for t in range(cuts):
                        piece = rows // cuts
                        copies.append(
                            pltpu.make_async_copy(
                                ref.at[batch, pl.ds(t * piece, piece), pl.ds(col, part)],
                                outs[place_out].at[
                                    pl.ds((2 * n + i) * rows + t * piece, piece), pl.ds(j * part, part)
                                ],
                                sem.at[place_out, j, 2 * n + i, t],
                            )
                        )
                        copies[-1].start()
    if extras:
        (batch,) = batches
        small = [
            pltpu.make_async_copy(source, target, small_sem.at[i])
            for i, (source, target) in enumerate(
                ((latent_ref.at[batch], latent), (beta_ref.at[batch], beta), (mark_ref, mark), (kind_ref, kind))
            )
        ]
        for c in small:
            c.start()
        for c in small:
            c.wait()
        lanes = width // 128
        misc = misc_rows(heads)
        wide[...] = beta[...].astype(f32)
        tokens = jnp.concatenate([mark[batch : batch + 1].astype(f32), kind[batch : batch + 1].astype(f32)], axis=0)
        for place_out, k in enumerate(ways):
            own = wide[pl.ds(pl.multiple_of((lo ^ k) * heads, heads), heads), :]
            values = jnp.concatenate([own, tokens, jnp.zeros((misc - heads - 2, rows), f32)], axis=0)
            values = jnp.concatenate([values, jnp.zeros((misc, 128 - rows), f32)], axis=1).astype(bf16)
            chunks = [latent[16 * j : 16 * j + 16] for j in range(rows // 16)]
            chunks += [values[16 * j : 16 * j + 16] for j in range(misc // 16)]
            chunks += [jnp.zeros((16, 128), bf16)] * (-len(chunks) % lanes)
            for c, chunk in enumerate(chunks):
                at = 2 * rows + 16 * (c // lanes)
                outs[place_out][at : at + 16, (c % lanes) * 128 : (c % lanes + 1) * 128] = chunk
    for c in copies:
        c.wait()


def pack_q_kernel(sub, batches, query_ref, *rest):
    outs, sem = rest[-sub - 1 : -1], rest[-1]
    lo = lax.rem(lax.axis_index("head"), sub)
    rows, width = query_ref.shape[1], query_ref.shape[2] // sub
    copies = []
    for k in range(sub):
        col = pl.multiple_of((lo ^ k) * width, width)
        for b in range(batches):
            copies.append(
                pltpu.make_async_copy(
                    query_ref.at[b, :, pl.ds(col, width)], outs[k].at[pl.ds(b * rows, rows)], sem.at[k, b]
                )
            )
            copies[-1].start()
    for c in copies:
        c.wait()


def exchange(pieces):
    count = lax.axis_size("head")
    got = {
        k: lax.ppermute(pieces[k], "head", [(i, i ^ k) for i in range(count)]) for k in range(len(pieces) - 1, 0, -1)
    }
    return [pieces[0]] + [got[k] for k in range(1, len(pieces))]


def place(outer, first, share, hp):
    at = pl.program_id(0) * hp
    hi = lax.div(lax.axis_index("head"), lax.axis_size("head") // outer)
    return (hi ^ (first + lax.div(at, share))) * share + lax.rem(at, share)


def reorder(parts, place, bits):
    for bit in range(bits):
        flipped = lax.rem(lax.div(place, 2**bit), 2) == 1
        parts = [jnp.where(flipped, parts[i ^ 2**bit], parts[i]) for i in range(len(parts))]
    return parts


def token_rows(pieces, slot, lo, tok, load):
    per = BLOCK // tok
    parts = [load(pieces[slot * per + r]) for r in range(per)]
    return jnp.concatenate(reorder(parts, lax.rem(lo, per), per.bit_length() - 1), axis=0)


def state_kernel(sub, outer, first, lane, blocks, heads, tok, hp, decay_ref, *rest):
    pieces, extras = rest[:sub], rest[sub : 2 * sub]
    up_ref, bias_ref = rest[2 * sub : 2 * sub + 2]
    w_ref, u_ref, shrink_ref, growth_ref, opre_ref, mpre_ref, span_ref, mask_ref, alive_ref = rest[-14:-5]
    levels, kinds, lasts, values, gates = rest[-5:]
    me = lax.rem(lax.axis_index("head"), sub)
    start = place(outer, first, heads // outer, hp)
    width = heads * DK
    per = BLOCK // tok
    row = lax.broadcasted_iota(jnp.int32, (BLOCK, BLOCK), 0)
    col = lax.broadcasted_iota(jnp.int32, (BLOCK, BLOCK), 1)
    low = (row >= col).astype(f32)
    low_b = low.astype(bf16)
    up_b = (row <= col).astype(bf16)
    unit_mat = (row == col).astype(bf16)
    count = BLOCK.bit_length() - 1
    step = pl.program_id(0)

    @pl.when(step == 0)
    def _():
        for level in range(count):
            size = 2**level
            here = (row // size == col // size + 1) & ((row // size) % 2 == 1)
            levels[level] = here.astype(bf16)
        lanes = extras[0].shape[1] // 128
        misc = misc_rows(heads)

        def chunk(piece, c):
            at = 2 * tok + 16 * (c // lanes)
            return piece[at : at + 16, (c % lanes) * 128 : (c % lanes + 1) * 128]

        for n in range(blocks):
            parts = [
                jnp.concatenate(
                    [chunk(extras[n * per + r], tok // 16 + j).astype(f32) for j in range(misc // 16)], axis=0
                )[:, :tok]
                for r in range(per)
            ]
            tall = jnp.concatenate(reorder(parts, lax.rem(me, per), per.bit_length() - 1), axis=1)
            values[n] = jax.nn.sigmoid(tall)
            mark = tall[heads : heads + 1]
            two = jnp.transpose(jnp.concatenate([tall[heads : heads + 2], jnp.zeros((6, BLOCK), f32)], axis=0))
            own = dot(low_b, jnp.broadcast_to(two[:, 0:1], (BLOCK, BLOCK)))
            other = dot(jnp.broadcast_to(mark, (BLOCK, BLOCK)), up_b)
            mask_ref[n] = jnp.where(own == other, low, 0.0)
            alive_ref[n] = (own == 0).astype(f32)
            lasts[n] = (own == other[:, BLOCK - 1 : BLOCK]).astype(f32)
            kinds[n] = jnp.broadcast_to(two[:, 1:2], (BLOCK, BLOCK))
            gates[n] = token_rows(
                extras, n, me, tok, lambda p: jnp.concatenate([chunk(p, j) for j in range(tok // 16)], axis=0)
            )

    low2 = jnp.concatenate([low_b, low_b], axis=1)
    lower = (row > col).astype(f32)
    items = [(i, n) for i in range(hp) for n in range(blocks)]
    every = range(blocks)
    strict_all, rhs_all, tail_all, carry_all = {}, {}, {}, {}
    betas = []
    for n in range(blocks):
        mine = values[n, pl.ds(start, hp), :]
        betas.append(jnp.transpose(jnp.concatenate([mine, jnp.zeros((8 - hp % 8, BLOCK), f32)], axis=0)))
    for i in range(hp):
        h = start + i
        at = pl.ds(pl.multiple_of(lane + (step * hp + i) * DK, DK), DK)
        bias_at = pl.ds(pl.multiple_of(me * width + h * DK, DK), DK)
        audio, text = bias_ref[0:1, bias_at], bias_ref[1:2, bias_at]
        rate = -LOG2E * jnp.exp(jnp.full((1, DK), decay_ref[me * heads + h], f32))
        for n in range(blocks):
            gate = dot(gates[n], up_ref[:, bias_at]).astype(bf16).astype(f32)
            pre = gate + jnp.where(kinds[n] == 1.0, text, audio)
            soft = jnp.maximum(pre, 0.0) + jnp.log(1.0 + jnp.exp(-jnp.abs(pre)))
            high, rest_part = split(rate * soft)
            total = dot(low2, jnp.concatenate([high, rest_part], axis=0))
            key = token_rows(pieces, n, me, tok, lambda p: p[0:tok, at]).astype(f32)
            value = token_rows(pieces, n, me, tok, lambda p: p[tok : 2 * tok, at]).astype(f32)
            unit = key * lax.rsqrt(jnp.sum(key * key, axis=1, keepdims=True) + norm_eps)
            growth = jnp.exp2(total)
            grown = unit * growth
            shrunk, shrunk_rest = split(unit * jnp.exp2(-total))
            last = total[BLOCK - 1 : BLOCK]
            tail = unit * (jnp.exp2(last - total) * lasts[n])
            carry = jnp.exp2(last) * alive_ref[n, BLOCK - 1 : BLOCK]
            beta = jnp.broadcast_to(betas[n][:, i : i + 1], (BLOCK, BLOCK))
            growth_ref[i, n] = growth
            shrink_ref[i, n, :, :DK] = shrunk
            shrink_ref[i, n, :, DK:] = shrunk_rest
            gram = dot(grown, shrunk, NT)
            strict_all[i, n] = (gram * (mask_ref[n] * lower) * beta).astype(bf16)
            rhs_all[i, n] = jnp.concatenate([beta * grown * alive_ref[n], beta * value], axis=1)
            tail_all[i, n] = jnp.transpose(tail)
            carry_all[i, n] = carry
    turned = jnp.transpose(jnp.concatenate([carry_all[t] for t in items] + [jnp.zeros((BLOCK - len(items), DK), f32)]))
    carry_all = {t: turned[:, j : j + 1] for j, t in enumerate(items)}
    inv = {t: unit_mat - strict_all[t] * levels[0] for t in items}
    for level in range(1, count):
        size = 2**level
        corner = {t: strict_all[t] * levels[level] for t in items}
        if size < 16:
            turn = {t: dot(inv[t], corner[t]) for t in items}
            inv = {t: inv[t] - dot(turn[t], inv[t]).astype(bf16) for t in items}
        else:
            pairs = BLOCK // (2 * size)
            four = {t: inv[t].reshape(pairs, 2, size, BLOCK) for t in items}
            odd = {t: four[t][:, 1].reshape(BLOCK // 2, BLOCK) for t in items}
            turn = {t: dot(odd[t], corner[t]) for t in items}
            odd = {t: odd[t] - dot(turn[t], inv[t]).astype(bf16) for t in items}
            inv = {
                t: jnp.stack([four[t][:, 0], odd[t].reshape(pairs, size, BLOCK)], axis=1).reshape(BLOCK, BLOCK)
                for t in items
            }
    both = {t: rhs_all[t] + dot(inv[t] - unit_mat, rhs_all[t]) for t in items}
    fade, offs = {}, {}
    for t in items:
        i, n = t
        w = both[t][:, :DK].astype(bf16)
        w_ref[i, n] = w
        u_ref[i, n] = both[t][:, DK:]
        uh, ul = split(both[t][:, DK:])
        th, tl = split(tail_all[t])
        joint = dot(th, jnp.concatenate([w, uh], axis=1))
        fade[t] = joint[:, :DK].astype(bf16)
        offs[t] = joint[:, DK:] + dot(jnp.concatenate([th, tl], axis=1), jnp.concatenate([ul, uh], axis=0))
    bits = blocks.bit_length() - 1
    for i in range(hp):
        for made in (fade, offs, carry_all):
            in_time = reorder([made[i, n] for n in every], lax.div(me, per), bits)
            for n in every:
                made[i, n] = in_time[n]
    offset = {i: offs[i, 0] for i in range(hp)}
    move = {i: jnp.where(row == col, carry_all[i, 0], 0.0) - fade[i, 0].astype(f32) for i in range(hp)}
    for n in range(1, blocks):
        for i in range(hp):
            opre_ref[i, n - 1] = offset[i]
            mpre_ref[i, n - 1] = move[i].astype(bf16)
            joint = dot(fade[i, n], jnp.concatenate([offset[i], move[i]], axis=1))
            offset[i] = carry_all[i, n] * offset[i] + offs[i, n] - joint[:, :DK]
            move[i] = carry_all[i, n] * move[i] - joint[:, DK:]
    for i in range(hp):
        span_ref[i] = jnp.concatenate([offset[i], move[i]], axis=1).astype(bf16)


def joined(later, earlier):
    both = dot(later[1], jnp.concatenate([earlier[0], earlier[1]], axis=1))
    return (later[0].astype(f32) + both[:, :DK]).astype(bf16), both[:, DK:].astype(bf16)


def ordered(outer, parts, order):
    hi = lax.div(lax.axis_index("head"), lax.axis_size("head") // outer)
    for j in range(outer):
        order[hi ^ j] = parts[j][...]


def compose_kernel(outer, share, *rest):
    parts, out_ref, order = rest[:outer], rest[-2], rest[-1]
    ordered(outer, parts, order)
    for h in range(share):
        whole = (order[0, h, :, :DK], order[0, h, :, DK:])
        for o in range(1, outer):
            whole = joined((order[o, h, :, :DK], order[o, h, :, DK:]), whole)
        out_ref[h, :, :DK] = whole[0]
        out_ref[h, :, DK:] = whole[1]


def relay_kernel(share, whole_ref, got_ref, *rest):
    out_ref = rest[-1]
    for h in range(share):
        whole = joined(
            (whole_ref[h, :, :DK], whole_ref[h, :, DK:]), (got_ref[h, :, :DK], got_ref[h, :, DK:])
        )
        out_ref[h, :, :DK] = whole[0]
        if out_ref.shape[2] > DK:
            out_ref[h, :, DK:] = whole[1]


def seed_kernel(outer, share, raw, *rest):
    parts = rest[:outer]
    early_ref, in_ref = rest[outer : outer + 2]
    outs, (order, seeds) = rest[-outer - 2 : -2], rest[-2:]
    hi = lax.div(lax.axis_index("head"), lax.axis_size("head") // outer)
    ordered(outer, parts, order)
    row = lax.broadcasted_iota(jnp.int32, (DK, DK), 0)
    col = lax.broadcasted_iota(jnp.int32, (DK, DK), 1)
    odd = lax.rem(lax.axis_index("seq"), 2) == 1
    for h in range(share):
        incoming = in_ref[h]
        through = dot(early_ref[h, :, DK:], incoming)
        if raw:
            through = jnp.where(odd, through, incoming.astype(f32))
        state = (early_ref[h, :, :DK].astype(f32) + through).astype(bf16)
        seeds[0, h] = state
        for o in range(1, outer):
            moved = dot(order[o - 1, h, :, DK:], state)
            state = (order[o - 1, h, :, :DK].astype(f32) + moved).astype(bf16)
            seeds[o, h] = state
    for j in range(outer):
        outs[j][...] = seeds[hi ^ j]


def query_kernel(sub, outer, first, blocks, heads, tok, batch, hp, *rest):
    pieces = rest[:sub]
    w_ref, u_ref, shrink_ref, growth_ref, mask_ref, alive_ref = rest[sub : sub + 6]
    base_ref, rows_ref = rest[-2:]
    lo = lax.rem(lax.axis_index("head"), sub)
    items = [(i, n) for i in range(hp) for n in range(blocks)]
    start = place(outer, first, heads // outer, hp)
    at = [pl.ds(pl.multiple_of((start + i) * DK, DK), DK) for i in range(hp)]
    grown, mix = {}, {}
    for i, n in items:
        query = token_rows(pieces, n, lo, tok, lambda p: p[batch * tok : (batch + 1) * tok, at[i]]).astype(f32)
        unit = query * (lax.rsqrt(jnp.sum(query * query, axis=1, keepdims=True) + norm_eps) * DK ** (-0.5))
        grown[i, n] = unit * growth_ref[i, n]
        gh, gl = split(grown[i, n])
        shrunk = shrink_ref[i, n]
        mix[i, n] = mask_ref[n] * dot(
            jnp.concatenate([gh, gh, gl], axis=1), jnp.concatenate([shrunk, shrunk[:, :DK]], axis=1), NT
        )
    for i, n in items:
        mh, ml = split(mix[i, n])
        uh, ul = split(u_ref[i, n])
        both = dot(mh, jnp.concatenate([uh, w_ref[i, n]], axis=1))
        rest_part = dot(jnp.concatenate([mh, ml], axis=1), jnp.concatenate([ul, uh], axis=0))
        base_ref[i, n] = both[:, :DK] + rest_part
        rows_ref[i, n] = (grown[i, n] * alive_ref[n] - both[:, DK:]).astype(bf16)


def output_kernel(sub, outer, sets, blocks, heads, tok, slots, *rest):
    seeds, rest = rest[:outer], rest[outer:]
    per = BLOCK // tok
    outs = rest[-len(slots) * per :]
    lo = lax.rem(lax.axis_index("head"), sub)
    hi = lax.div(lax.axis_index("head"), sub)
    share = heads // outer
    for part, (first, shares) in enumerate(sets):
        base_ref, rows_ref, opre_ref, mpre_ref = rest[4 * part : 4 * part + 4]
        for r in range(shares * share):
            j, i = first + r // share, r % share
            at = pl.ds(pl.multiple_of(((hi ^ j) * share + i) * DK, DK), DK)
            seed = seeds[j][i]
            states = [seed] + [
                (opre_ref[r, n] + dot(mpre_ref[r, n], seed)).astype(bf16) for n in range(blocks - 1)
            ]
            states = reorder(states, lax.div(lo, per), blocks.bit_length() - 1)
            for m, n in enumerate(slots):
                core = (base_ref[r, n] + dot(rows_ref[r, n], states[n])).astype(bf16)
                rows = reorder([core[t * tok : (t + 1) * tok] for t in range(per)], lax.rem(lo, per), per.bit_length() - 1)
                for t in range(per):
                    outs[m * per + t][:, at] = rows[t]


def finish_kernel(sub, heads, *rest):
    pieces = rest[:sub]
    gate_ref, gain_ref = rest[sub : sub + 2]
    out_ref = rest[-1]
    me = lax.rem(lax.axis_index("head"), sub)
    for k in range(sub):
        for h in range(heads):
            at = pl.ds(pl.multiple_of((me ^ k) * (heads * DK) + h * DK, DK), DK)
            core = pieces[k][:, h * DK : (h + 1) * DK].astype(f32)
            normed = core * lax.rsqrt(jnp.mean(core * core, axis=1, keepdims=True) + norm_eps)
            out_ref[0, :, at] = (normed * gain_ref[:, at] * jax.nn.sigmoid(gate_ref[0, :, at].astype(f32))).astype(bf16)


def product(a, b):
    return jnp.einsum("hij,hjk->hik", a, b, preferred_element_type=f32)


def before(span, *after):
    count = lax.axis_size("seq")
    place = lax.axis_index("seq")
    unit_mat = jnp.broadcast_to(jnp.eye(DK, dtype=bf16), span.shape[:1] + (DK, DK))
    raw = True
    early, whole = None, span
    size = 1
    while size < count:
        final = 2 * size >= count
        payload = whole[..., :DK] if final and size == 1 else whole
        got = None
        for t in range(size):
            pairs = [
                (base + size - 1, base + size + t)
                for base in range(0, count, 2 * size)
                if base + size + t < count
            ]
            part = lax.ppermute(payload, "seq", pairs)
            got = part if got is None else got + part
        if final:
            break
        right = (place // size) % 2 == 1
        if size == 1:
            early = got
        else:
            e_move = early[..., DK:]
            if raw:
                e_move = jnp.where(place % 2 == 1, e_move, unit_mat)
            raw = False
            moved = product(e_move, got)
            early = jnp.concatenate(
                [
                    (early[..., :DK].astype(f32) + moved[..., :DK]).astype(bf16),
                    jnp.where(right, moved[..., DK:].astype(bf16), e_move),
                ],
                axis=2,
            )
        share = whole.shape[0]
        last = 4 * size >= count
        whole = pl.pallas_call(
            functools.partial(relay_kernel, share),
            out_shape=jax.ShapeDtypeStruct((share, DK, DK if last else 2 * DK), bf16),
            in_specs=[VMEM] * 2 + [ANY] * len(after),
            out_specs=VMEM,
            compiler_params=params(16),
            cost_estimate=cost(0, 0),
            name=f"relay_{size}",
        )(whole, got, *after)
        size *= 2
    if early is None:
        early = jnp.concatenate([jnp.zeros_like(unit_mat), unit_mat], axis=2)
    return early, got, raw


def per_device(
    query_rows,
    key_rows,
    value_rows,
    beta_raw,
    gate_latent,
    gate_up,
    dt_bias,
    decay_log,
    boundary,
    modality,
    out_gate,
    norm_gain,
):
    places = lax.axis_size("head")
    batches, tok, columns = query_rows.shape
    sub = min(places, 4)
    outer = places // sub
    total_heads = columns // DK
    heads = total_heads // sub
    share = heads // outer
    width = heads * DK
    blocks = tok * sub // BLOCK
    sds = jax.ShapeDtypeStruct
    by_head_t = jnp.swapaxes(beta_raw, 1, 2)
    sets = ([(1, outer - 1)] if outer > 1 else []) + [(0, 1)]
    misc = tok // 16 + misc_rows(heads) // 16

    def pack_kv(of, first, shares, extras, ways, direct, *after):
        lanes = shares * share
        rows = 2 * tok * len(of) + (16 * -(-misc // lanes) if extras else 0)
        return pl.pallas_call(
            functools.partial(pack_kv_kernel, sub, ways, outer, of, heads, first, extras),
            out_shape=[sds((rows, lanes * DK), bf16)] * len(ways),
            in_specs=[ANY] * (6 + len(after)),
            out_specs=[VMEM] * len(ways),
            scratch_shapes=[
                pltpu.VMEM(gate_latent.shape[1:], bf16),
                pltpu.VMEM(by_head_t.shape[1:], bf16),
                pltpu.VMEM(boundary.shape, jnp.int32),
                pltpu.VMEM(modality.shape, jnp.int32),
                pltpu.VMEM(by_head_t.shape[1:], f32),
                pltpu.SemaphoreType.DMA((len(ways), shares, 2 * len(of), max(1, tok // 16) if direct else 1)),
                pltpu.SemaphoreType.DMA((4,)),
            ],
            compiler_params=params(60 if direct else 16),
            cost_estimate=cost(0, 0),
            name=f"pack_kv_{of[0]}_{ways[0]}",
        )(key_rows, value_rows, gate_latent, by_head_t, boundary, modality, *after)

    hp = min(share, max(1, 8 // blocks))
    while share % hp:
        hp -= 1
    before_rows = max(1, blocks - 1)

    def by_head(*dims):
        return pl.BlockSpec((hp, *dims), lambda i: (i,) + (0,) * len(dims))

    per_head = by_head(blocks, DK, DK)
    wide_head = by_head(blocks, DK, 2 * DK)
    pre_head = by_head(before_rows, DK, DK)
    whole = pl.BlockSpec((blocks, BLOCK, BLOCK), lambda i: (0, 0, 0))
    levels = BLOCK.bit_length() - 1
    local_dims = [
        ((blocks, DK, DK), bf16),
        ((blocks, DK, DK), f32),
        ((blocks, DK, 2 * DK), bf16),
        ((blocks, DK, DK), f32),
        ((before_rows, DK, DK), f32),
        ((before_rows, DK, DK), bf16),
        ((DK, 2 * DK), bf16),
    ]
    count = lax.axis_size("head")

    def state_maps(b, part, *after):
        first, shares = sets[part]
        pieces = extras = kv[b]
        lane = sum(earlier for _, earlier in sets[:part]) * share * DK
        here = shares * share
        return pl.pallas_call(
            functools.partial(state_kernel, sub, outer, first, lane, blocks, heads, tok, hp),
            grid=(here // hp,),
            out_shape=[sds((here, *dims), kind) for dims, kind in local_dims] + [sds((blocks, BLOCK, BLOCK), f32)] * 2,
            in_specs=[SMEM] + [VMEM] * (2 * sub + 2) + [ANY] * len(after),
            out_specs=[by_head(*dims) for dims, _ in local_dims] + [whole, whole],
            scratch_shapes=[
                pltpu.VMEM((levels, BLOCK, BLOCK), bf16),
                pltpu.VMEM((blocks, BLOCK, BLOCK), f32),
                pltpu.VMEM((blocks, BLOCK, BLOCK), f32),
                pltpu.VMEM((blocks, misc_rows(heads), BLOCK), f32),
                pltpu.VMEM((blocks, BLOCK, BLOCK), bf16),
            ],
            compiler_params=params(),
            cost_estimate=cost(SCALE * here * blocks * 2e8, 0),
            name=f"state_maps_{b}_{first}",
        )(decay_log, *pieces, *extras, gate_up, dt_bias, *after)

    def swap(parts):
        return [parts[0]] + [
            lax.ppermute(parts[j], "head", [(i, i ^ (j * sub)) for i in range(count)]) for j in range(1, outer)
        ]

    def pack_q(*after):
        return pl.pallas_call(
            functools.partial(pack_q_kernel, sub, batches),
            out_shape=[sds((batches * tok, width), bf16)] * sub,
            in_specs=[ANY] * (1 + len(after)),
            out_specs=[VMEM] * sub,
            scratch_shapes=[pltpu.SemaphoreType.DMA((sub, batches))],
            compiler_params=params(16),
            cost_estimate=cost(0, 0),
            name="pack_q",
        )(query_rows, *after)

    def query_parts(b, part, *after):
        first, shares = sets[part]
        here = local[b][part]
        return pl.pallas_call(
            functools.partial(query_kernel, sub, outer, first, blocks, heads, tok, b, hp),
            grid=(shares * share // hp,),
            out_shape=[
                sds((shares * share, blocks, DK, DK), f32),
                sds((shares * share, blocks, DK, DK), bf16),
            ],
            in_specs=[VMEM] * sub + [per_head, per_head, wide_head, per_head] + [whole] * 2 + [ANY] * len(after),
            out_specs=[per_head] * 2,
            compiler_params=params(),
            cost_estimate=cost(SCALE * shares * share * blocks * 1e8, 0),
            name=f"query_parts_{b}_{first}",
        )(*q_here, *here[:4], *here[7:9], *after)

    def compose(b, parts, *after):
        return pl.pallas_call(
            functools.partial(compose_kernel, outer, share),
            out_shape=sds((share, DK, 2 * DK), bf16),
            in_specs=[VMEM] * outer + [ANY] * len(after),
            out_specs=VMEM,
            scratch_shapes=[pltpu.VMEM((outer, share, DK, 2 * DK), bf16)],
            compiler_params=params(),
            cost_estimate=cost(0, 0),
            name=f"compose_{b}",
        )(*parts, *after)

    def seeds(b, parts, early, incoming, raw, *after):
        return pl.pallas_call(
            functools.partial(seed_kernel, outer, share, raw),
            out_shape=[sds((share, DK, DK), bf16)] * outer,
            in_specs=[VMEM] * (outer + 2) + [ANY] * len(after),
            out_specs=[VMEM] * outer,
            scratch_shapes=[
                pltpu.VMEM((outer, share, DK, 2 * DK), bf16),
                pltpu.VMEM((outer, share, DK, DK), bf16),
            ],
            compiler_params=params(16),
            cost_estimate=cost(0, 0),
            name=f"seeds_{b}",
        )(*parts, early, incoming, *after)

    def outputs(b, queries, given):
        operands = []
        for made, here in zip(queries, local[b]):
            operands += [*made, *here[4:6]]
        pieces = {}
        per = sub // blocks
        near = (blocks + 1) // 2
        after = []
        for slots in (list(range(near, blocks)), list(range(near))):
            if not slots:
                continue
            made = pl.pallas_call(
                functools.partial(output_kernel, sub, outer, sets, blocks, heads, tok, slots),
                out_shape=[sds((tok, width), bf16)] * (len(slots) * per),
                in_specs=[VMEM] * (len(operands) + outer) + [ANY] * len(after),
                out_specs=[VMEM] * (len(slots) * per),
                compiler_params=params(),
                cost_estimate=cost(SCALE * heads * len(slots) * 2e7, 0),
                name=f"span_outputs_{b}_{slots[0]}",
            )(*given, *operands, *after)
            after = [made[0]]
            for m, n in enumerate(slots):
                for t in range(per):
                    pieces[n * per + t] = made[m * per + t]
        return [pieces[k] for k in range(sub)]

    def swapped(made):
        sent = []
        if outer > 1:
            spans = made[0][6]
            sent = [spans] if outer == 2 else [spans[j * share : (j + 1) * share] for j in range(outer - 1)]
        return swap([made[-1][6]] + sent)

    parts_here = range(len(sets))
    jobs = [(b, part) for part in parts_here for b in range(batches)]
    local = [[None] * len(sets) for _ in range(batches)]
    queries = [[] for _ in range(batches)]
    moved, totals, begins, outs, back, relays = {}, {}, {}, {}, [], {}
    token = None
    kv = []
    for b in range(batches):
        if b == 0:
            far = pack_kv([b], sets[0][0], outer, True, [sub - 1], True)
            packed = pack_kv([b], sets[0][0], outer, True, list(range(sub - 1)), True, far[0]) + far if sub > 1 else far
        else:
            packed = pack_kv([b], sets[0][0], outer, True, list(range(sub)), False, token)
        kv.append(exchange(packed))
        token = kv[b][-1]
    packed_q = pack_q(token)
    q_here = exchange(packed_q)
    token = packed[0]
    for b, part in jobs:
        local[b][part] = state_maps(b, part, token)
    for b in range(batches):
        moved[b] = swapped(local[b])
    def chain(b, *after):
        totals[b] = compose(b, moved[b], *after)
        relays[b] = before(totals[b])
        begins[b] = seeds(b, moved[b], *relays[b])

    last = batches - 1
    for part in parts_here:
        queries[last].append(query_parts(last, part))
    for b in range(batches):
        chain(b, *([made[1] for made in queries[last]] if b == last else []))
    for b in range(last):
        for part in parts_here:
            queries[b].append(query_parts(b, part))
    for b in range(batches):
        outs[b] = outputs(b, queries[b], swap(begins[b]))
        back.append(exchange(outs[b]))

    mixed = None
    for b in range(batches):
        rows = pl.BlockSpec((1, tok, columns), lambda i, b=b: (b, 0, 0))
        mixed = pl.pallas_call(
            functools.partial(finish_kernel, sub, heads),
            grid=(1,),
            out_shape=sds((batches, tok, columns), bf16),
            in_specs=[pl.BlockSpec((tok, width), lambda i: (0, 0))] * sub
            + [rows, pl.BlockSpec((1, columns), lambda i: (0, 0))]
            + ([] if b == 0 else [ANY]),
            out_specs=rows,
            input_output_aliases={} if b == 0 else {sub + 2: 0},
            compiler_params=params(),
            cost_estimate=cost(0, 0),
            name=f"finish_{b}",
        )(*back[b], out_gate, norm_gain[None, :], *([] if b == 0 else [mixed]))
    return mixed


def solution(mesh):
    return jax.shard_map(
        per_device,
        mesh=mesh,
        in_specs=(
            P(None, ("seq", "head"), None),
            P(None, ("seq", "head"), None),
            P(None, ("seq", "head"), None),
            P(None, ("seq", "head"), None),
            P(None, ("seq", "head"), None),
            P(),
            P(),
            P(),
            P(None, ("seq", "head")),
            P(None, ("seq", "head")),
            P(None, ("seq", "head"), None),
            P(),
        ),
        out_specs=P(None, ("seq", "head"), None),
        check_vma=False,
    )
```
